128 devices in a mesh: row: 4 (over z_hi, core), tm: 32 (over y, z_lo, x).
Axes of the slice: x: 4, y: 4, z: 4 (z_hi: 2, z_lo: 2; z = z_hi * 2 + z_lo), core: 2. Of those that a mesh axis runs over, the one named last changes fastest.
Arguments:
- temps: bfloat16 [24576, 16384], P('row', 'tm')
- area: float32 [24576], P('row'), may hold values from 0.2 to 1
- ocean_rows: int32 [24576], P('row'), may hold values from 0 to 6143, as said below
- counts: int32 [4], P('row'), may hold values from 1536 to 6144, as said below
Outputs:
- band: float32 [2048, 16384], P('row', 'tm')
The draws below stay inside these ranges and needn't reach their ends.
Inputs may be any that keep to these rules, and one draw needn't show every extreme that they name: `ocean_rows`: within each tile of 6144 entries, every local row number appears once. `counts`: some tile is all ocean.
All inputs are finite; a program needn't handle non-finite values.
Results may differ from the reference program's by a relative error of at most 0.0022.
Values may be sent and summed in bfloat16 or wider, within the bound.
A program may use at most 64 MiB of HBM per device.

```python
import math
import jax
import jax.numpy as jnp
from jax import lax

ROW_DEV = 6144
HOUR_DEV = 512
LAGS = 4
ROWS = 24576
HOURS = 16384
N_ROW = 4
N_TM = 32


def draw_temps(key, part):
    key = jax.random.fold_in(key, 11)
    offset_key, noise_key = jax.random.split(key, 2)
    offsets = jax.random.uniform(offset_key, (ROWS, 1), jnp.float32, -3.0, 3.0)
    noise = jax.random.normal(noise_key, (ROWS, HOURS), jnp.float32)
    values = offsets + noise
    return jnp.clip(values, -12.0, 12.0).astype(jnp.bfloat16)


def draw_ocean_rows(key, part):
    key = jax.random.fold_in(key, 23)
    tiles = jnp.arange(N_ROW, dtype=jnp.int32)
    lists = jax.vmap(lambda tile: jax.random.permutation(jax.random.fold_in(key, tile), ROW_DEV))(tiles)
    return lists.reshape(-1).astype(jnp.int32)


def draw_counts(key, part):
    key = jax.random.fold_in(key, 37)
    first_key, second_key = jax.random.split(key)
    values = jax.random.randint(first_key, (N_ROW,), ROW_DEV // 4, ROW_DEV + 1, jnp.int32)
    full_tile = jax.random.randint(second_key, (), 0, N_ROW, jnp.int32)
    return values.at[full_tile].set(ROW_DEV).astype(jnp.int32)


def shard_levels(stream_key, dims, cuts, low, largest):
    loudness = 1.0
    for axis_at, parts in cuts:
        draws = jax.random.uniform(jax.random.fold_in(jax.random.fold_in(stream_key, 6), axis_at), (parts,), jnp.float32, low / len(cuts), largest / len(cuts))
        loudness = loudness * jnp.repeat(jnp.exp(draws), dims[axis_at] // parts).reshape((-1,) + (1,) * (len(dims) - 1 - axis_at))
    return loudness


def setup_inputs(seed: int = 0) -> dict:
    key_of = jax.random.split(jax.random.key(seed), 5)
    temps = draw_temps(jax.random.fold_in(key_of[4], 71), 0)
    area = jnp.clip(jnp.exp(math.log(1.0) - 1.609438 * jax.random.uniform(key_of[1], (ROWS,), jnp.float32) ** shard_levels(key_of[1], (ROWS,), ((0, 4),), -0.2, 0.2)), 0.2, 1.0)
    ocean_rows = draw_ocean_rows(jax.random.fold_in(key_of[4], 71), 0)
    counts = draw_counts(jax.random.fold_in(key_of[4], 71), 0)
    return {"temps": temps, "area": area, "ocean_rows": ocean_rows, "counts": counts}


def reference(temps, area, ocean_rows, counts):
    sums = lax.optimization_barrier(jnp.sum(temps.astype(jnp.float32), axis=1))
    mean = sums / HOURS
    tile_rows = ocean_rows.reshape(N_ROW, ROW_DEV) + (jnp.arange(N_ROW, dtype=jnp.int32) * ROW_DEV)[:, None]
    live = (jnp.arange(ROW_DEV, dtype=jnp.int32)[None, :] < counts[:, None]).astype(jnp.float32)
    ocean = jnp.zeros((ROWS,), jnp.float32).at[tile_rows.reshape(-1)].set(live.reshape(-1))
    weighted = ((temps.astype(jnp.float32) - mean[:, None]) * (ocean * area)[:, None]).astype(jnp.bfloat16)
    blocks = jnp.transpose(weighted.reshape(ROWS, N_TM, HOUR_DEV), (1, 0, 2))

    def one_block(index):
        own = lax.dynamic_index_in_dim(blocks, index, 0, keepdims=False)
        pieces = []
        for lag in range(LAGS):
            other = lax.dynamic_index_in_dim(blocks, (index + lag) % N_TM, 0, keepdims=False)
            pieces.append(jnp.dot(other.T, own, preferred_element_type=jnp.float32))
        return jnp.concatenate(pieces, axis=0)
    stacked = lax.map(one_block, jnp.arange(N_TM, dtype=jnp.int32))
    band = jnp.transpose(stacked, (1, 0, 2)).reshape(LAGS * HOUR_DEV, HOURS)
    return band / jnp.sqrt(jnp.float32(ROWS))
```

```python
import functools
import math

import jax
import jax.numpy as jnp
from jax import lax
from jax.experimental import pallas as pl
from jax.experimental.pallas import tpu as pltpu
from jax.sharding import PartitionSpec as P

LAGS = 4
NX = 4
NG = 8
LANES = 128
CHUNK = 256
EARLY = 3
MESH = pl.DeviceIdType.MESH
F32 = jnp.float32
BF16 = jnp.bfloat16
CROSS_ROWS = (((0,), (0,)), ((), ()))
CROSS_LANES = (((1,), (1,)), ((), ()))
PAIRS = (
    [(i, k) for i in range(NX) for k in range(LAGS) if i + k < NX],
    [(1, 3), (2, 2), (3, 1)],
    [(2, 3), (3, 2)],
    [(3, 3)],
)


def kernel(
    temps, area, listed, count, out,
    raw, halo, weighted, own, csend, crecv, xsend, xrecv, zsend, zrecv,
    sums, near, partial, far, means, scales, local_sem,
    xs_sem, xr_sem, hs_sem, hr_sem, cs_sem, cr_sem, ps_sem, pr_sem, zs_sem, zr_sem,
    ns_sem, nr_sem, fs_sem, fr_sem,
):
    row, tm = lax.axis_index("row"), lax.axis_index("tm")
    zh, core = row // 2, lax.rem(row, 2)
    group, x = tm // NX, lax.rem(tm, NX)
    quarter = raw.shape[1]
    chunks = quarter // CHUNK
    tiles = quarter // LANES
    hours = raw.shape[2]

    def x_peer(step):
        return (row, group * NX + lax.rem(x + step, NX))

    def g_peer(step):
        return (row, lax.rem(group + step, NG) * NX + x)

    partner = (zh * 2 + 1 - core, tm)
    opposite = (lax.rem(row + 2, 4), tm)
    x_at = [lax.rem(x + step, NX) for step in range(NX)]

    barrier = pltpu.get_barrier_semaphore()
    everyone = [x_peer(s) for s in range(1, NX)] + [g_peer(s) for s in range(1, NG)]
    everyone += [partner, opposite]
    for device in everyone:
        pl.semaphore_signal(barrier, inc=1, device_id=device, device_id_type=MESH)

    def remote(src, dst, send, recv, device):
        return pltpu.make_async_remote_copy(
            src_ref=src, dst_ref=dst, send_sem=send, recv_sem=recv, device_id=device, device_id_type=MESH
        )

    def rows_of(piece, base=0):
        return pl.ds(pl.multiple_of(base + piece * CHUNK, CHUNK), CHUNK)

    stage = [
        pltpu.make_async_copy(
            temps.at[pl.ds(q * quarter, quarter)], weighted.at[q], local_sem.at[q]
        )
        for q in range(NX)
    ]
    keep = pltpu.make_async_copy(
        temps.at[pl.ds(pl.multiple_of(x * quarter, quarter), quarter)], raw.at[x], local_sem.at[NX]
    )
    for copy in stage:
        copy.start()
    keep.start()

    def exchange(step, piece):
        target = x_at[step]
        return remote(
            temps.at[rows_of(piece, target * quarter)], raw.at[x, rows_of(piece)],
            xs_sem.at[step - 1, piece], xr_sem.at[NX - step - 1, piece], x_peer(step),
        )

    def arrival(step, piece):
        source = x_at[step]
        return remote(
            temps.at[rows_of(piece)], raw.at[source, rows_of(piece)],
            xs_sem.at[0, 0], xr_sem.at[step - 1, piece], x_peer(step),
        )

    def forward(block, piece):
        return remote(
            raw.at[block, rows_of(piece)], halo.at[block, rows_of(piece)],
            hs_sem.at[block, piece], hr_sem.at[block, piece], g_peer(NG - 1),
        )

    def forward_own(piece):
        return remote(
            temps.at[rows_of(piece, x * quarter)], halo.at[x, rows_of(piece)],
            hs_sem.at[x, piece], hr_sem.at[x, piece], g_peer(NG - 1),
        )

    pl.semaphore_wait(barrier, len(everyone))

    for piece in range(chunks):
        exchange(1, piece).start()
        exchange(3, piece).start()
    for piece in range(chunks):
        @pl.when((x < 2) | ((x == 2) & (piece < EARLY)))
        def _():
            forward_own(piece).start()
    for piece in range(chunks):
        exchange(2, piece).start()

    sums[...] = jnp.zeros_like(sums)
    ones = jnp.ones((8, hours), BF16)
    for q in range(NX):
        stage[q].wait()
        for piece in range(quarter // 512):
            some = lax.dot_general(
                ones, weighted[q, pl.ds(piece * 512, 512)], CROSS_LANES, preferred_element_type=F32
            )
            for part in range(4):
                sums[q, pl.ds(piece * 4 + part, 1)] = some[0:1, part * LANES : (part + 1) * LANES]
    keep.wait()

    def send_near(step):
        return remote(
            sums.at[x_at[step]], near.at[NX - step - 1], ns_sem.at[step - 1], nr_sem.at[NX - step - 1], x_peer(step)
        )

    def send_far(step):
        return remote(partial, far.at[NG - step - 1], fs_sem.at[step - 1], fr_sem.at[NG - step - 1], g_peer(step))

    for step in range(1, NX):
        send_near(step).start()

    per = listed.shape[1]
    live = count[0]
    mask = jnp.zeros((16, LANES), F32)
    for part in range(listed.shape[0]):
        value = listed[pl.ds(part, 1), :]
        high = jnp.broadcast_to(value // LANES - x * tiles, (16, per))
        low = jnp.broadcast_to(value % LANES, (LANES, per))
        place = lax.broadcasted_iota(jnp.int32, (LANES, per), 1) + part * per
        left = jnp.where(high == lax.broadcasted_iota(jnp.int32, (16, per), 0), 1.0, 0.0).astype(BF16)
        hit = (low == lax.broadcasted_iota(jnp.int32, (LANES, per), 0)) & (place < live)
        right = jnp.where(hit, 1.0, 0.0).astype(BF16)
        mask = mask + lax.dot_general(left, right, CROSS_LANES, preferred_element_type=F32)
    scale = mask[:tiles] * area[x]

    def spread(row_values, target):
        for a in range(tiles):
            target[pl.ds(a * LANES, LANES)] = jnp.broadcast_to(row_values[a : a + 1], (LANES, LANES)).T

    spread(scale, scales)

    def pass_on(step, piece):
        arrival(step, piece).wait_recv()
        @pl.when(x_at[step] < NX - 1)
        def _():
            forward(x_at[step], piece).start()

    for piece in range(2):
        pass_on(3, piece)
        pass_on(1, piece)

    for step in range(1, NX):
        send_near(step).wait_recv()
    partial[...] = sums[x] + near[0] + near[1] + near[2]
    for step in range(1, NG):
        send_far(step).start()

    for piece in range(2, chunks):
        pass_on(3, piece)
        pass_on(1, piece)

    for step in range(1, NG):
        send_far(step).wait_recv()
    total = partial[...]
    for step in range(NG - 1):
        total = total + far[step]
    spread(total[:tiles] / (hours * NX * NG), means)

    def weigh(source, target, piece):
        r = rows_of(piece)
        m, s = means[r], scales[r]
        for lane in range(0, hours, LANES):
            at = pl.ds(lane, LANES)
            target[r, at] = ((source[r, at].astype(F32) - m) * s).astype(BF16)

    for piece in range(chunks):
        pass_on(2, piece)
        for step in (0, 1, 3):
            weigh(raw.at[x_at[step]], weighted.at[x_at[step]], piece)
        weigh(raw.at[x_at[2]], weighted.at[x_at[2]], piece)
    for piece in range(EARLY, chunks):
        @pl.when(x == 2)
        def _():
            forward_own(piece).start()

    def slot_of(i, k):
        return i * 2 + k // 2

    def swap(slot):
        return remote(csend.at[slot], crecv.at[slot], cs_sem.at[slot], cr_sem.at[slot], partner)

    def to_owner(i, k):
        away = lax.rem(x - i + NX, NX)
        at = lax.rem(away + NX - 1, NX)
        return remote(
            xsend.at[slot_of(i, k)], xrecv.at[at, k // 2],
            ps_sem.at[slot_of(i, k)], pr_sem.at[at, k // 2], (row, group * NX + i),
        )

    def multiply(i, k):
        value = lax.dot_general(weighted[i + k], weighted[i], CROSS_ROWS, preferred_element_type=F32)
        slot = slot_of(i, k)
        mine = core == k % 2

        @pl.when(mine)
        def _():
            own[slot] = value

        @pl.when(jnp.logical_not(mine))
        def _():
            csend[slot] = value
            swap(slot).start()

    def finish(i, k):
        slot = slot_of(i, k)

        @pl.when(core == k % 2)
        def _():
            swap(slot).wait_recv()

            @pl.when(x == i)
            def _():
                own[slot] = own[slot] + crecv[slot]

            @pl.when(x != i)
            def _():
                xsend[slot] = (own[slot] + crecv[slot]).astype(BF16)
                to_owner(i, k).start()

    waiting = []
    for stage_at, pairs in enumerate(PAIRS):
        if stage_at:
            block = stage_at - 1
            for piece in range(chunks):
                forward(block, piece).wait_recv()
                weigh(halo.at[block], weighted.at[NX + block], piece)
        for pair in pairs:
            multiply(*pair)
            waiting.append(pair)
            if len(waiting) > 2:
                finish(*waiting.pop(0))
    for pair in waiting:
        finish(*pair)

    def gathered(kk):
        for d in range(NX - 1):
            remote(
                xsend.at[0], xrecv.at[d, kk], ps_sem.at[0], pr_sem.at[d, kk], x_peer(d + 1)
            ).wait_recv()
        value = own[x * 2 + kk]
        for d in range(NX - 1):
            value = value + xrecv[d, kk].astype(F32)
        return value

    across = remote(zsend, zrecv, zs_sem, zr_sem, opposite)
    zsend[...] = gathered(1 - zh).astype(BF16)
    across.start()
    mine = gathered(zh)
    across.wait_recv()
    out[...] = (mine + zrecv[...].astype(F32)) / math.sqrt(quarter * NX * 4)

    for step in range(1, NX):
        for piece in range(chunks):
            exchange(step, piece).wait_send()
        send_near(step).wait_send()
    for step in range(1, NG):
        send_far(step).wait_send()
    for block in range(NX - 1):
        for piece in range(chunks):
            forward(block, piece).wait_send()
    for i in range(NX):
        for k in range(LAGS):
            slot = slot_of(i, k)

            @pl.when(core != k % 2)
            def _():
                swap(slot).wait_send()

            @pl.when((core == k % 2) & (x != i))
            def _():
                to_owner(i, k).wait_send()
    across.wait_send()


def body(temps, area, ocean_rows, counts):
    rows, hours = temps.shape
    quarter = rows // NX
    chunks = quarter // CHUNK
    vmem = pl.BlockSpec(memory_space=pltpu.VMEM)
    dma = pltpu.SemaphoreType.DMA
    return pl.pallas_call(
        kernel,
        out_shape=jax.ShapeDtypeStruct((hours, hours), F32),
        in_specs=[
            pl.BlockSpec(memory_space=pl.ANY), vmem, vmem, pl.BlockSpec(memory_space=pltpu.SMEM),
        ],
        out_specs=vmem,
        scratch_shapes=[
            pltpu.VMEM((NX, quarter, hours), BF16),
            pltpu.VMEM((NX - 1, quarter, hours), BF16),
            pltpu.VMEM((2 * NX - 1, quarter, hours), BF16),
            pltpu.VMEM((2 * NX, hours, hours), F32),
            pltpu.VMEM((2 * NX, hours, hours), F32),
            pltpu.VMEM((2 * NX, hours, hours), F32),
            pltpu.VMEM((2 * NX, hours, hours), BF16),
            pltpu.VMEM((NX - 1, 2, hours, hours), BF16),
            pltpu.VMEM((hours, hours), BF16),
            pltpu.VMEM((hours, hours), BF16),
            pltpu.VMEM((NX, 16, LANES), F32),
            pltpu.VMEM((NX - 1, 16, LANES), F32),
            pltpu.VMEM((16, LANES), F32),
            pltpu.VMEM((NG - 1, 16, LANES), F32),
            pltpu.VMEM((quarter, LANES), F32),
            pltpu.VMEM((quarter, LANES), F32),
            dma((NX + 1,)),
            dma((NX - 1, chunks)), dma((NX - 1, chunks)),
            dma((NX - 1, chunks)), dma((NX - 1, chunks)),
            dma((2 * NX,)), dma((2 * NX,)),
            dma((2 * NX,)), dma((NX - 1, 2)),
            dma, dma,
            dma((NX - 1,)), dma((NX - 1,)),
            dma((NG - 1,)), dma((NG - 1,)),
        ],
        compiler_params=pltpu.CompilerParams(
            collective_id=0, has_side_effects=True, vmem_limit_bytes=62 << 20
        ),
        cost_estimate=pl.CostEstimate(
            flops=2 * LAGS * hours * hours * rows, bytes_accessed=2 * rows * hours, transcendentals=0
        ),
        name="lagged_band",
    )(temps, area.reshape(NX, -1, LANES), ocean_rows.reshape(8, -1), counts)


def solution(mesh):
    in_specs = (P("row", "tm"), P("row"), P("row"), P("row"))
    out_specs = P("row", "tm")
    return jax.shard_map(body, mesh=mesh, in_specs=in_specs, out_specs=out_specs, check_vma=False)
```

```python
import functools
import math

import jax
import jax.numpy as jnp
from jax import lax
from jax.experimental import pallas as pl
from jax.experimental.pallas import tpu as pltpu
from jax.sharding import PartitionSpec as P

LAGS = 4
NX = 4
NG = 8
LANES = 128
CHUNK = 256
EARLY = 2
WINDOW = 3
MESH = pl.DeviceIdType.MESH
F32 = jnp.float32
BF16 = jnp.bfloat16
CROSS_ROWS = (((0,), (0,)), ((), ()))
CROSS_LANES = (((1,), (1,)), ((), ()))
PAIRS = (
    [(i, k) for i in range(NX) for k in range(LAGS) if i + k < NX],
    [(1, 3), (2, 2), (3, 1)],
    [(2, 3), (3, 2)],
    [(3, 3)],
)


def kernel(
    temps, area, listed, count, out,
    raw, halo, weighted, own, csend, crecv, xsend, xrecv, zsend, zrecv,
    sums, near, partial, far, scale, means, scales, local_sem,
    xs_sem, xr_sem, hs_sem, hr_sem, cs_sem, cr_sem, ps_sem, pr_sem, zs_sem, zr_sem,
    ns_sem, nr_sem, fs_sem, fr_sem,
):
    row, tm = lax.axis_index("row"), lax.axis_index("tm")
    zh, core = row // 2, lax.rem(row, 2)
    group, x = tm // NX, lax.rem(tm, NX)
    quarter = raw.shape[1]
    chunks = quarter // CHUNK
    tiles = quarter // LANES
    hours = raw.shape[2]

    def x_peer(step):
        return (row, group * NX + lax.rem(x + step, NX))

    def g_peer(step):
        return (row, lax.rem(group + step, NG) * NX + x)

    partner = (zh * 2 + 1 - core, tm)
    opposite = (lax.rem(row + 2, 4), tm)
    x_at = [lax.rem(x + step, NX) for step in range(NX)]

    barrier = pltpu.get_barrier_semaphore()
    everyone = [x_peer(s) for s in range(1, NX)] + [g_peer(s) for s in range(1, NG)]
    everyone += [partner, opposite]
    for device in everyone:
        pl.semaphore_signal(barrier, inc=1, device_id=device, device_id_type=MESH)

    def remote(src, dst, send, recv, device):
        return pltpu.make_async_remote_copy(
            src_ref=src, dst_ref=dst, send_sem=send, recv_sem=recv, device_id=device, device_id_type=MESH
        )

    def rows_of(piece, base=0):
        return pl.ds(pl.multiple_of(base + piece * CHUNK, CHUNK), CHUNK)

    stage = [
        pltpu.make_async_copy(
            temps.at[pl.ds(q * quarter, quarter)], weighted.at[q], local_sem.at[q]
        )
        for q in range(NX)
    ]
    keep = pltpu.make_async_copy(
        temps.at[pl.ds(pl.multiple_of(x * quarter, quarter), quarter)], raw.at[x], local_sem.at[NX]
    )
    for copy in stage:
        copy.start()
    keep.start()

    def exchange(step, piece):
        target = x_at[step]
        return remote(
            temps.at[rows_of(piece, target * quarter)], raw.at[x, rows_of(piece)],
            xs_sem.at[step - 1, piece], xr_sem.at[NX - step - 1, piece], x_peer(step),
        )

    def arrival(step, piece):
        source = x_at[step]
        return remote(
            temps.at[rows_of(piece)], raw.at[source, rows_of(piece)],
            xs_sem.at[0, 0], xr_sem.at[step - 1, piece], x_peer(step),
        )

    def forward(block, piece):
        return remote(
            raw.at[block, rows_of(piece)], halo.at[block, rows_of(piece)],
            hs_sem.at[block, piece], hr_sem.at[block, piece], g_peer(NG - 1),
        )

    def forward_own(piece):
        return remote(
            temps.at[rows_of(piece, x * quarter)], halo.at[x, rows_of(piece)],
            hs_sem.at[x, piece], hr_sem.at[x, piece], g_peer(NG - 1),
        )

    pl.semaphore_wait(barrier, len(everyone))

    for piece in range(WINDOW):
        exchange(1, piece).start()
        exchange(3, piece).start()
    for piece in range(chunks):
        @pl.when((x == 0) | ((x < NX - 1) & (piece < EARLY)))
        def _():
            forward_own(piece).start()

    sums[...] = jnp.zeros_like(sums)
    ones = jnp.ones((8, hours), BF16)
    for q in range(NX):
        stage[q].wait()
        for piece in range(quarter // 512):
            some = lax.dot_general(
                ones, weighted[q, pl.ds(piece * 512, 512)], CROSS_LANES, preferred_element_type=F32
            )
            for part in range(4):
                sums[q, pl.ds(piece * 4 + part, 1)] = some[0:1, part * LANES : (part + 1) * LANES]
    keep.wait()

    def send_near(step):
        return remote(
            sums.at[x_at[step]], near.at[NX - step - 1], ns_sem.at[step - 1], nr_sem.at[NX - step - 1], x_peer(step)
        )

    def send_far(step):
        return remote(partial, far.at[NG - step - 1], fs_sem.at[step - 1], fr_sem.at[NG - step - 1], g_peer(step))

    for step in range(1, NX):
        send_near(step).start()

    def one_hop(piece):
        arrival(3, piece).wait_recv()
        arrival(1, piece).wait_recv()

        @pl.when((x == 1) | (x == 2))
        def _():
            forward(x - 1, piece).start()

        @pl.when(x == 3)
        def _():
            forward(0, piece).start()

        if piece < EARLY:
            @pl.when(x == 3)
            def _():
                forward(2, piece).start()
        if piece + WINDOW < chunks:
            exchange(1, piece + WINDOW).start()
            exchange(3, piece + WINDOW).start()
        else:
            some = chunks // WINDOW
            for late in range(some):
                exchange(2, (piece + WINDOW - chunks) * some + late).start()

    one_hop(0)

    live = count[0]
    groups = listed.shape[0]

    def mark(part, mask):
        value = listed[pl.ds(part, 1), :]
        high = jnp.broadcast_to(value // LANES, (groups, LANES))
        low = jnp.broadcast_to(value % LANES, (LANES, LANES))
        place = lax.broadcasted_iota(jnp.int32, (LANES, LANES), 1) + part * LANES
        left = jnp.where(high == lax.broadcasted_iota(jnp.int32, (groups, LANES), 0), 1.0, 0.0).astype(BF16)
        hit = (low == lax.broadcasted_iota(jnp.int32, (LANES, LANES), 0)) & (place < live)
        right = jnp.where(hit, 1.0, 0.0).astype(BF16)
        return mask + lax.dot_general(left, right, CROSS_LANES, preferred_element_type=F32)

    mask = lax.fori_loop(0, groups, mark, jnp.zeros((groups, LANES), F32))
    scale[...] = mask * area[...]

    def spread(row_of, target):
        for a in range(tiles):
            target[pl.ds(a * LANES, LANES)] = jnp.broadcast_to(row_of(a), (LANES, LANES)).T

    spread(lambda a: scale[pl.ds(x * tiles + a, 1)], scales)

    one_hop(1)
    for step in range(1, NX):
        send_near(step).wait_recv()
    partial[...] = sums[x] + near[0] + near[1] + near[2]
    for step in range(1, NG):
        send_far(step).start()

    for piece in range(2, chunks):
        one_hop(piece)

    for piece in range(chunks):
        @pl.when(x == 0)
        def _():
            forward(1, piece).start()
        if piece >= EARLY:
            @pl.when(x == 1)
            def _():
                forward_own(piece).start()

    for step in range(1, NG):
        send_far(step).wait_recv()
    total = partial[...]
    for step in range(NG - 1):
        total = total + far[step]
    mean = total[:tiles] / (hours * NX * NG)
    spread(lambda a: mean[a : a + 1], means)

    def weigh(source, target, piece):
        r = rows_of(piece)
        m, s = means[r], scales[r]
        for lane in range(0, hours, LANES):
            at = pl.ds(lane, LANES)
            target[r, at] = ((source[r, at].astype(F32) - m) * s).astype(BF16)

    for piece in range(chunks):
        for step in (0, 1, 3):
            weigh(raw.at[x_at[step]], weighted.at[x_at[step]], piece)
        arrival(2, piece).wait_recv()

        @pl.when(x != 1)
        def _():
            forward(x_at[2], piece).start()
        weigh(raw.at[x_at[2]], weighted.at[x_at[2]], piece)
    for piece in range(chunks):
        @pl.when(x == 1)
        def _():
            forward(2, piece).start()
        if piece >= EARLY:
            @pl.when(x == 2)
            def _():
                forward_own(piece).start()

            @pl.when(x == 3)
            def _():
                forward(2, piece).start()

    def slot_of(i, k):
        return i * 2 + k // 2

    def swap(slot):
        return remote(csend.at[slot], crecv.at[slot], cs_sem.at[slot], cr_sem.at[slot], partner)

    def to_owner(i, k):
        away = lax.rem(x - i + NX, NX)
        at = lax.rem(away + NX - 1, NX)
        return remote(
            xsend.at[slot_of(i, k)], xrecv.at[at, k // 2],
            ps_sem.at[slot_of(i, k)], pr_sem.at[at, k // 2], (row, group * NX + i),
        )

    def multiply(i, k):
        value = lax.dot_general(weighted[i + k], weighted[i], CROSS_ROWS, preferred_element_type=F32)
        slot = slot_of(i, k)
        mine = core == k % 2

        @pl.when(mine)
        def _():
            own[slot] = value

        @pl.when(jnp.logical_not(mine))
        def _():
            csend[slot] = value
            swap(slot).start()

    def finish(i, k):
        slot = slot_of(i, k)

        @pl.when(core == k % 2)
        def _():
            swap(slot).wait_recv()

            @pl.when(x == i)
            def _():
                own[slot] = own[slot] + crecv[slot]

            @pl.when(x != i)
            def _():
                xsend[slot] = (own[slot] + crecv[slot]).astype(BF16)
                to_owner(i, k).start()

    waiting = []
    for stage_at, pairs in enumerate(PAIRS):
        if stage_at:
            block = stage_at - 1
            for piece in range(chunks):
                forward(block, piece).wait_recv()
                weigh(halo.at[block], weighted.at[NX + block], piece)
        for pair in pairs:
            multiply(*pair)
            waiting.append(pair)
            if len(waiting) > 2:
                finish(*waiting.pop(0))
        while waiting:
            finish(*waiting.pop(0))

    def gathered(kk):
        for d in range(NX - 1):
            remote(
                xsend.at[0], xrecv.at[d, kk], ps_sem.at[0], pr_sem.at[d, kk], x_peer(d + 1)
            ).wait_recv()
        value = own[x * 2 + kk]
        for d in range(NX - 1):
            value = value + xrecv[d, kk].astype(F32)
        return value

    across = remote(zsend, zrecv, zs_sem, zr_sem, opposite)
    zsend[...] = gathered(1 - zh).astype(BF16)
    across.start()
    mine = gathered(zh)
    across.wait_recv()
    out[...] = (mine + zrecv[...].astype(F32)) / math.sqrt(quarter * NX * 4)

    for step in range(1, NX):
        for piece in range(chunks):
            exchange(step, piece).wait_send()
        send_near(step).wait_send()
    for step in range(1, NG):
        send_far(step).wait_send()
    for block in range(NX - 1):
        for piece in range(chunks):
            forward(block, piece).wait_send()
    for i in range(NX):
        for k in range(LAGS):
            slot = slot_of(i, k)

            @pl.when(core != k % 2)
            def _():
                swap(slot).wait_send()

            @pl.when((core == k % 2) & (x != i))
            def _():
                to_owner(i, k).wait_send()
    across.wait_send()


def body(temps, area, ocean_rows, counts):
    rows, hours = temps.shape
    quarter = rows // NX
    chunks = quarter // CHUNK
    vmem = pl.BlockSpec(memory_space=pltpu.VMEM)
    dma = pltpu.SemaphoreType.DMA
    return pl.pallas_call(
        kernel,
        out_shape=jax.ShapeDtypeStruct((hours, hours), F32),
        in_specs=[
            pl.BlockSpec(memory_space=pl.ANY), vmem, vmem, pl.BlockSpec(memory_space=pltpu.SMEM),
        ],
        out_specs=vmem,
        scratch_shapes=[
            pltpu.VMEM((NX, quarter, hours), BF16),
            pltpu.VMEM((NX - 1, quarter, hours), BF16),
            pltpu.VMEM((2 * NX - 1, quarter, hours), BF16),
            pltpu.VMEM((2 * NX, hours, hours), F32),
            pltpu.VMEM((2 * NX, hours, hours), F32),
            pltpu.VMEM((2 * NX, hours, hours), F32),
            pltpu.VMEM((2 * NX, hours, hours), BF16),
            pltpu.VMEM((NX - 1, 2, hours, hours), BF16),
            pltpu.VMEM((hours, hours), BF16),
            pltpu.VMEM((hours, hours), BF16),
            pltpu.VMEM((NX, 16, LANES), F32),
            pltpu.VMEM((NX - 1, 16, LANES), F32),
            pltpu.VMEM((16, LANES), F32),
            pltpu.VMEM((NG - 1, 16, LANES), F32),
            pltpu.VMEM((rows // LANES, LANES), F32),
            pltpu.VMEM((quarter, LANES), F32),
            pltpu.VMEM((quarter, LANES), F32),
            dma((NX + 1,)),
            dma((NX - 1, chunks)), dma((NX - 1, chunks)),
            dma((NX - 1, chunks)), dma((NX - 1, chunks)),
            dma((2 * NX,)), dma((2 * NX,)),
            dma((2 * NX,)), dma((NX - 1, 2)),
            dma, dma,
            dma((NX - 1,)), dma((NX - 1,)),
            dma((NG - 1,)), dma((NG - 1,)),
        ],
        compiler_params=pltpu.CompilerParams(
            collective_id=0, has_side_effects=True, vmem_limit_bytes=62 << 20
        ),
        cost_estimate=pl.CostEstimate(
            flops=2 * LAGS * hours * hours * rows, bytes_accessed=2 * rows * hours, transcendentals=0
        ),
        name="lagged_band",
    )(temps, area.reshape(-1, LANES), ocean_rows.reshape(-1, LANES), counts)


def solution(mesh):
    in_specs = (P("row", "tm"), P("row"), P("row"), P("row"))
    out_specs = P("row", "tm")
    return jax.shard_map(body, mesh=mesh, in_specs=in_specs, out_specs=out_specs, check_vma=False)
```

```python
import functools
import math

import jax
import jax.numpy as jnp
from jax import lax
from jax.experimental import pallas as pl
from jax.experimental.pallas import tpu as pltpu
from jax.sharding import PartitionSpec as P

LAGS = 4
NX = 4
NG = 8
LANES = 128
CHUNK = 256
EARLY = 2
WINDOW = 3
MESH = pl.DeviceIdType.MESH
F32 = jnp.float32
BF16 = jnp.bfloat16
CROSS_ROWS = (((0,), (0,)), ((), ()))
CROSS_LANES = (((1,), (1,)), ((), ()))
PARTS = 2


def without(x, with_far):
    far = (x + 2) % NX
    pairs = [(i, k) for k in range(LAGS) for i in range(NX) if i + k < NX]
    return [(i, k) for i, k in pairs if (far in (i, i + k)) == with_far]


EARLY_PAIRS = list(zip(*[without(x, False) for x in range(NX)]))
LATE_PAIRS = list(zip(*[without(x, True) for x in range(NX)]))
CROSS_PAIRS = [[(1, 3), (2, 2), (3, 1)], [(2, 3), (3, 2)], [(3, 3)]]


def kernel(
    temps, area, listed, count, out,
    raw, halo, weighted, own, csend, crecv, xsend, xrecv, zsend, zrecv,
    sums, near, partial, far, scale, means, scales, local_sem,
    xs_sem, xr_sem, hs_sem, hr_sem, cs_sem, cr_sem, ps_sem, pr_sem, zs_sem, zr_sem,
    ns_sem, nr_sem, fs_sem, fr_sem,
):
    row, tm = lax.axis_index("row"), lax.axis_index("tm")
    zh, core = row // 2, lax.rem(row, 2)
    group, x = tm // NX, lax.rem(tm, NX)
    quarter = raw.shape[1]
    chunks = quarter // CHUNK
    tiles = quarter // LANES
    hours = raw.shape[2]
    half = hours // PARTS

    def x_peer(step):
        return (row, group * NX + lax.rem(x + step, NX))

    def g_peer(step):
        return (row, lax.rem(group + step, NG) * NX + x)

    partner = (zh * 2 + 1 - core, tm)
    opposite = (lax.rem(row + 2, 4), tm)
    x_at = [lax.rem(x + step, NX) for step in range(NX)]

    barrier = pltpu.get_barrier_semaphore()
    everyone = [x_peer(s) for s in range(1, NX)] + [g_peer(s) for s in range(1, NG)]
    everyone += [partner, opposite]
    for device in everyone:
        pl.semaphore_signal(barrier, inc=1, device_id=device, device_id_type=MESH)

    def remote(src, dst, send, recv, device):
        return pltpu.make_async_remote_copy(
            src_ref=src, dst_ref=dst, send_sem=send, recv_sem=recv, device_id=device, device_id_type=MESH
        )

    def rows_of(piece, base=0):
        return pl.ds(pl.multiple_of(base + piece * CHUNK, CHUNK), CHUNK)

    stage = [
        pltpu.make_async_copy(
            temps.at[pl.ds(q * quarter, quarter)], weighted.at[q], local_sem.at[q]
        )
        for q in range(NX)
    ]
    keep = pltpu.make_async_copy(
        temps.at[pl.ds(pl.multiple_of(x * quarter, quarter), quarter)], raw.at[x], local_sem.at[NX]
    )
    for copy in stage:
        copy.start()
    keep.start()

    def exchange(step, piece):
        target = x_at[step]
        return remote(
            temps.at[rows_of(piece, target * quarter)], raw.at[x, rows_of(piece)],
            xs_sem.at[step - 1, piece], xr_sem.at[NX - step - 1, piece], x_peer(step),
        )

    def arrival(step, piece):
        source = x_at[step]
        return remote(
            temps.at[rows_of(piece)], raw.at[source, rows_of(piece)],
            xs_sem.at[0, 0], xr_sem.at[step - 1, piece], x_peer(step),
        )

    def forward(block, piece):
        return remote(
            raw.at[block, rows_of(piece)], halo.at[block, rows_of(piece)],
            hs_sem.at[block, piece], hr_sem.at[block, piece], g_peer(NG - 1),
        )

    def forward_own(piece):
        return remote(
            temps.at[rows_of(piece, x * quarter)], halo.at[x, rows_of(piece)],
            hs_sem.at[x, piece], hr_sem.at[x, piece], g_peer(NG - 1),
        )

    pl.semaphore_wait(barrier, len(everyone))

    for piece in range(WINDOW):
        exchange(1, piece).start()
        exchange(3, piece).start()
    for piece in range(chunks):
        @pl.when((x == 0) | ((x < NX - 1) & (piece < EARLY)))
        def _():
            forward_own(piece).start()

    sums[...] = jnp.zeros_like(sums)
    ones = jnp.ones((8, hours), BF16)
    for q in range(NX):
        stage[q].wait()
        for piece in range(quarter // 512):
            some = lax.dot_general(
                ones, weighted[q, pl.ds(piece * 512, 512)], CROSS_LANES, preferred_element_type=F32
            )
            for part in range(4):
                sums[q, pl.ds(piece * 4 + part, 1)] = some[0:1, part * LANES : (part + 1) * LANES]
    keep.wait()

    def send_near(step):
        return remote(
            sums.at[x_at[step]], near.at[NX - step - 1], ns_sem.at[step - 1], nr_sem.at[NX - step - 1], x_peer(step)
        )

    def send_far(step):
        return remote(partial, far.at[NG - step - 1], fs_sem.at[step - 1], fr_sem.at[NG - step - 1], g_peer(step))

    for step in range(1, NX):
        send_near(step).start()

    def one_hop(piece):
        arrival(3, piece).wait_recv()
        arrival(1, piece).wait_recv()

        @pl.when((x == 1) | (x == 2))
        def _():
            forward(x - 1, piece).start()

        @pl.when(x == 3)
        def _():
            forward(0, piece).start()

        if piece < EARLY:
            @pl.when(x == 3)
            def _():
                forward(2, piece).start()
        if piece + WINDOW < chunks:
            exchange(1, piece + WINDOW).start()
            exchange(3, piece + WINDOW).start()
        else:
            some = chunks // WINDOW
            for late in range(some):
                exchange(2, (piece + WINDOW - chunks) * some + late).start()

    one_hop(0)

    live = count[0]
    groups = listed.shape[0]

    def mark(part, mask):
        value = listed[pl.ds(part, 1), :]
        high = jnp.broadcast_to(value // LANES, (groups, LANES))
        low = jnp.broadcast_to(value % LANES, (LANES, LANES))
        place = lax.broadcasted_iota(jnp.int32, (LANES, LANES), 1) + part * LANES
        left = jnp.where(high == lax.broadcasted_iota(jnp.int32, (groups, LANES), 0), 1.0, 0.0).astype(BF16)
        hit = (low == lax.broadcasted_iota(jnp.int32, (LANES, LANES), 0)) & (place < live)
        right = jnp.where(hit, 1.0, 0.0).astype(BF16)
        return mask + lax.dot_general(left, right, CROSS_LANES, preferred_element_type=F32)

    mask = lax.fori_loop(0, groups, mark, jnp.zeros((groups, LANES), F32))
    scale[...] = mask * area[...]

    def spread(row_of, target):
        for a in range(tiles):
            target[pl.ds(a * LANES, LANES)] = jnp.broadcast_to(row_of(a), (LANES, LANES)).T

    spread(lambda a: scale[pl.ds(x * tiles + a, 1)], scales)

    one_hop(1)
    for step in range(1, NX):
        send_near(step).wait_recv()
    partial[...] = sums[x] + near[0] + near[1] + near[2]
    for step in range(1, NG):
        send_far(step).start()

    for piece in range(2, chunks):
        one_hop(piece)

    for piece in range(chunks):
        @pl.when(x == 0)
        def _():
            forward(1, piece).start()
        if piece >= EARLY:
            @pl.when(x == 1)
            def _():
                forward_own(piece).start()

    for step in range(1, NG):
        send_far(step).wait_recv()
    total = partial[...]
    for step in range(NG - 1):
        total = total + far[step]
    mean = total[:tiles] / (hours * NX * NG)
    spread(lambda a: mean[a : a + 1], means)

    def weigh(source, target, piece):
        r = rows_of(piece)
        m, s = means[r], scales[r]
        for lane in range(0, hours, LANES):
            at = pl.ds(lane, LANES)
            target[r, at] = ((source[r, at].astype(F32) - m) * s).astype(BF16)

    def pick(values):
        value = values[0]
        for at in range(1, NX):
            value = jnp.where(x == at, values[at], value)
        return value

    def lag_pair(pairs):
        return pick([i for i, _ in pairs]), pick([k for _, k in pairs])

    def slot_of(i, k):
        return i * 2 + k // 2

    def part_of(part):
        return pl.ds(part * half, half)

    def swap(slot, part):
        return remote(
            csend.at[slot, part_of(part)], crecv.at[slot, part_of(part)],
            cs_sem.at[slot, part], cr_sem.at[slot, part], partner,
        )

    def to_owner(i, k, part):
        away = lax.rem(x - i + NX, NX)
        at = lax.rem(away + NX - 1, NX)
        slot = slot_of(i, k)
        return remote(
            xsend.at[slot, part_of(part)], xrecv.at[at, k // 2, part_of(part)],
            ps_sem.at[slot, part], pr_sem.at[at, k // 2, part], (row, group * NX + i),
        )

    def multiply(i, k):
        slot = slot_of(i, k)
        mine = core == lax.rem(k, 2)
        for part in range(PARTS):
            value = lax.dot_general(
                weighted[i + k, :, part * half : (part + 1) * half], weighted[i],
                CROSS_ROWS, preferred_element_type=F32,
            )

            @pl.when(mine)
            def _():
                own[slot, part_of(part)] = value

            @pl.when(jnp.logical_not(mine))
            def _():
                csend[slot, part_of(part)] = value
                swap(slot, part).start()

    def finish(i, k):
        slot = slot_of(i, k)

        @pl.when(core == lax.rem(k, 2))
        def _():
            for part in range(PARTS):
                at = part_of(part)
                swap(slot, part).wait_recv()

                @pl.when(x == i)
                def _():
                    own[slot, at] = own[slot, at] + crecv[slot, at]

                @pl.when(x != i)
                def _():
                    xsend[slot, at] = (own[slot, at] + crecv[slot, at]).astype(BF16)
                    to_owner(i, k, part).start()

    for piece in range(chunks):
        for step in (0, 1, 3):
            weigh(raw.at[x_at[step]], weighted.at[x_at[step]], piece)
    early = [lag_pair(pairs) for pairs in EARLY_PAIRS]
    for piece in range(chunks):
        arrival(2, piece).wait_recv()

        @pl.when(x != 1)
        def _():
            forward(x_at[2], piece).start()
        weigh(raw.at[x_at[2]], weighted.at[x_at[2]], piece)
        if piece < len(early):
            multiply(*early[piece])
    for piece in range(chunks):
        @pl.when(x == 1)
        def _():
            forward(2, piece).start()
        if piece >= EARLY:
            @pl.when(x == 2)
            def _():
                forward_own(piece).start()

            @pl.when(x == 3)
            def _():
                forward(2, piece).start()

    waiting = early
    stages = [[lag_pair(pairs) for pairs in LATE_PAIRS]] + CROSS_PAIRS
    for stage_at, pairs in enumerate(stages):
        if stage_at:
            block = stage_at - 1
            for piece in range(chunks):
                forward(block, piece).wait_recv()
                weigh(halo.at[block], weighted.at[NX + block], piece)
        for pair in pairs:
            multiply(*pair)
            waiting.append(pair)
            while len(waiting) > 2:
                finish(*waiting.pop(0))
        if stage_at < len(stages) - 1:
            while waiting:
                finish(*waiting.pop(0))

    def gathered(kk, part):
        for d in range(NX - 1):
            remote(
                xsend.at[0, part_of(part)], xrecv.at[d, kk, part_of(part)],
                ps_sem.at[0, part], pr_sem.at[d, kk, part], x_peer(d + 1),
            ).wait_recv()
        value = own[x * 2 + kk, part_of(part)]
        for d in range(NX - 1):
            value = value + xrecv[d, kk, part_of(part)].astype(F32)
        return value

    def across(part):
        return remote(
            zsend.at[part_of(part)], zrecv.at[part_of(part)], zs_sem.at[part], zr_sem.at[part], opposite
        )

    def send_across():
        for part in range(PARTS):
            zsend[part_of(part)] = gathered(1 - zh, part).astype(BF16)
            across(part).start()

    last = (x == NX - 1) & (core == 1) & (zh == 0)

    @pl.when(jnp.logical_not(last))
    def _():
        send_across()
    while waiting:
        finish(*waiting.pop(0))

    @pl.when(last)
    def _():
        send_across()
    for part in range(PARTS):
        value = gathered(zh, part)
        across(part).wait_recv()
        out[part_of(part)] = (value + zrecv[part_of(part)].astype(F32)) / math.sqrt(quarter * NX * 4)

    for step in range(1, NX):
        for piece in range(chunks):
            exchange(step, piece).wait_send()
        send_near(step).wait_send()
    for step in range(1, NG):
        send_far(step).wait_send()
    for block in range(NX - 1):
        for piece in range(chunks):
            forward(block, piece).wait_send()
    for i in range(NX):
        for k in range(LAGS):
            for part in range(PARTS):
                @pl.when(core != k % 2)
                def _():
                    swap(slot_of(i, k), part).wait_send()

                @pl.when((core == k % 2) & (x != i))
                def _():
                    to_owner(i, k, part).wait_send()
    for part in range(PARTS):
        across(part).wait_send()


def body(temps, area, ocean_rows, counts):
    rows, hours = temps.shape
    quarter = rows // NX
    chunks = quarter // CHUNK
    vmem = pl.BlockSpec(memory_space=pltpu.VMEM)
    dma = pltpu.SemaphoreType.DMA
    return pl.pallas_call(
        kernel,
        out_shape=jax.ShapeDtypeStruct((hours, hours), F32),
        in_specs=[
            pl.BlockSpec(memory_space=pl.ANY), vmem, vmem, pl.BlockSpec(memory_space=pltpu.SMEM),
        ],
        out_specs=vmem,
        scratch_shapes=[
            pltpu.VMEM((NX, quarter, hours), BF16),
            pltpu.VMEM((NX - 1, quarter, hours), BF16),
            pltpu.VMEM((2 * NX - 1, quarter, hours), BF16),
            pltpu.VMEM((2 * NX, hours, hours), F32),
            pltpu.VMEM((2 * NX, hours, hours), F32),
            pltpu.VMEM((2 * NX, hours, hours), F32),
            pltpu.VMEM((2 * NX, hours, hours), BF16),
            pltpu.VMEM((NX - 1, 2, hours, hours), BF16),
            pltpu.VMEM((hours, hours), BF16),
            pltpu.VMEM((hours, hours), BF16),
            pltpu.VMEM((NX, 16, LANES), F32),
            pltpu.VMEM((NX - 1, 16, LANES), F32),
            pltpu.VMEM((16, LANES), F32),
            pltpu.VMEM((NG - 1, 16, LANES), F32),
            pltpu.VMEM((rows // LANES, LANES), F32),
            pltpu.VMEM((quarter, LANES), F32),
            pltpu.VMEM((quarter, LANES), F32),
            dma((NX + 1,)),
            dma((NX - 1, chunks)), dma((NX - 1, chunks)),
            dma((NX - 1, chunks)), dma((NX - 1, chunks)),
            dma((2 * NX, PARTS)), dma((2 * NX, PARTS)),
            dma((2 * NX, PARTS)), dma((NX - 1, 2, PARTS)),
            dma((PARTS,)), dma((PARTS,)),
            dma((NX - 1,)), dma((NX - 1,)),
            dma((NG - 1,)), dma((NG - 1,)),
        ],
        compiler_params=pltpu.CompilerParams(
            collective_id=0, has_side_effects=True, vmem_limit_bytes=62 << 20
        ),
        cost_estimate=pl.CostEstimate(
            flops=2 * LAGS * hours * hours * rows, bytes_accessed=2 * rows * hours, transcendentals=0
        ),
        name="lagged_band",
    )(temps, area.reshape(-1, LANES), ocean_rows.reshape(-1, LANES), counts)


def solution(mesh):
    in_specs = (P("row", "tm"), P("row"), P("row"), P("row"))
    out_specs = P("row", "tm")
    return jax.shard_map(body, mesh=mesh, in_specs=in_specs, out_specs=out_specs, check_vma=False)
```

```python
import functools
import math

import jax
import jax.numpy as jnp
from jax import lax
from jax.experimental import pallas as pl
from jax.experimental.pallas import tpu as pltpu
from jax.sharding import PartitionSpec as P

LAGS = 4
NX = 4
NG = 8
LANES = 128
CHUNK = 128
EARLY = 2
WINDOW = 6
BANDS = 3
MESH = pl.DeviceIdType.MESH
F32 = jnp.float32
BF16 = jnp.bfloat16
CROSS_ROWS = (((0,), (0,)), ((), ()))
CROSS_LANES = (((1,), (1,)), ((), ()))
PARTS = 2


NEAR_PAIRS = list(zip(
    [(1, 0), (3, 0), (1, 2), (0, 0), (0, 1), (0, 3)],
    [(0, 0), (2, 0), (0, 1), (0, 2), (1, 0), (1, 1)],
    [(1, 0), (3, 0), (1, 1), (1, 2), (2, 0), (2, 1)],
    [(0, 0), (2, 0), (0, 2), (2, 1), (0, 3), (3, 0)],
))
NEXT_PAIRS = list(zip(
    [(3, 1), (1, 3)],
    [(2, 2), (1, 3)],
    [(3, 2), (2, 3)],
    [(2, 2), (3, 1)],
))
FAR_PAIRS = list(zip(
    [(2, 0), (2, 1), (1, 1), (0, 2)],
    [(3, 0), (2, 1), (0, 3), (1, 2)],
    [(0, 0), (0, 1), (0, 2), (0, 3)],
    [(1, 0), (1, 1), (0, 1), (1, 2)],
))
THEN_PAIRS = list(zip(
    [(2, 2), (3, 2), (2, 3)],
    [(3, 1), (2, 3), (3, 2)],
    [(1, 3), (3, 1), (2, 2)],
    [(1, 3), (2, 3), (3, 2)],
))
LAST_PAIR = (3, 3)
OUT_AT = (5, 12, 15)


def crossing_first(pairs, zh):
    return sorted(pairs, key=lambda pair: pair[1] // 2 == zh)


def out_order(zh, x):
    def best(pool, taken):
        def rank(pair):
            i, k = pair
            since = [n for n, (owner, _) in enumerate(taken) if owner == i]
            return (i == x, k // 2 == zh, since[-1] if since else -1, pool.index(pair))

        return min(pool, key=rank)

    pool = [pairs[x] for pairs in NEAR_PAIRS + NEXT_PAIRS]
    taken = []
    for upto, more in zip(OUT_AT, (FAR_PAIRS, THEN_PAIRS, [])):
        while len(taken) < upto:
            pair = best(pool, taken)
            pool.remove(pair)
            taken.append(pair)
        pool += [pairs[x] for pairs in more]
    return taken


def by_place(order):
    return list(zip(*[order(zh, x) for zh in range(2) for x in range(NX)]))


OUT_PAIRS = by_place(out_order)
FAR_ORDER = by_place(lambda zh, x: crossing_first([pairs[x] for pairs in FAR_PAIRS], zh))
THEN_ORDER = by_place(lambda zh, x: crossing_first([pairs[x] for pairs in THEN_PAIRS], zh))


def kernel(
    temps, area, listed, count, out,
    raw, weighted, own, csend, crecv, xsend, xrecv, between, zsend, zrecv,
    sums, near, partial, far, scale, means, scales, local_sem,
    xs_sem, xr_sem, hs_sem, hr_sem, ls_sem, lr_sem, cs_sem, cr_sem, ps_sem, pr_sem, bs_sem, zs_sem, zr_sem,
    ns_sem, nr_sem, fs_sem, fr_sem,
):
    row, tm = lax.axis_index("row"), lax.axis_index("tm")
    zh, core = row // 2, lax.rem(row, 2)
    group, x = tm // NX, lax.rem(tm, NX)
    quarter = raw.shape[1]
    chunks = quarter // CHUNK
    tiles = quarter // LANES
    hours = raw.shape[2]
    half = hours // PARTS

    def x_peer(step):
        return (row, group * NX + lax.rem(x + step, NX))

    def g_peer(step):
        return (row, lax.rem(group + step, NG) * NX + x)

    partner = (zh * 2 + 1 - core, tm)
    opposite = (lax.rem(row + 2, 4), tm)
    x_at = [lax.rem(x + step, NX) for step in range(NX)]

    barrier = pltpu.get_barrier_semaphore()
    everyone = [x_peer(s) for s in range(1, NX)] + [g_peer(s) for s in range(1, NG)]
    everyone += [partner, opposite]
    for device in everyone:
        pl.semaphore_signal(barrier, inc=1, device_id=device, device_id_type=MESH)

    def remote(src, dst, send, recv, device):
        return pltpu.make_async_remote_copy(
            src_ref=src, dst_ref=dst, send_sem=send, recv_sem=recv, device_id=device, device_id_type=MESH
        )

    def rows_of(piece, base=0):
        return pl.ds(pl.multiple_of(base + piece * CHUNK, CHUNK), CHUNK)

    stage = [
        pltpu.make_async_copy(
            temps.at[pl.ds(q * quarter, quarter)], weighted.at[q], local_sem.at[q]
        )
        for q in range(NX)
    ]
    keep = pltpu.make_async_copy(
        temps.at[pl.ds(pl.multiple_of(x * quarter, quarter), quarter)], raw.at[x], local_sem.at[NX]
    )
    for copy in stage:
        copy.start()
    keep.start()

    def exchange(step, piece):
        target = x_at[step]
        return remote(
            temps.at[rows_of(piece, target * quarter)], raw.at[x, rows_of(piece)],
            xs_sem.at[step - 1, piece], xr_sem.at[NX - step - 1, piece], x_peer(step),
        )

    def arrival(step, piece):
        source = x_at[step]
        return remote(
            temps.at[rows_of(piece)], raw.at[source, rows_of(piece)],
            xs_sem.at[0, 0], xr_sem.at[step - 1, piece], x_peer(step),
        )

    def forward(block, piece):
        return remote(
            raw.at[block, rows_of(piece)], weighted.at[NX + block, rows_of(piece)],
            hs_sem.at[block, piece], hr_sem.at[block, piece], g_peer(NG - 1),
        )

    def forward_own(piece):
        return remote(
            temps.at[rows_of(piece, x * quarter)], weighted.at[NX + x, rows_of(piece)],
            hs_sem.at[x, piece], hr_sem.at[x, piece], g_peer(NG - 1),
        )

    band = quarter // BANDS

    def forward_last(part, at, mine=False):
        r, cols = pl.ds(at * band, band), pl.ds(part * half, half)
        source = raw.at[2, r, cols]
        if mine:
            source = temps.at[pl.ds(pl.multiple_of(x * quarter + at * band, band), band), cols]
        return remote(
            source, weighted.at[NX + 2, r, cols], ls_sem.at[part, at], lr_sem.at[part, at], g_peer(NG - 1)
        )

    pl.semaphore_wait(barrier, len(everyone))

    for piece in range(WINDOW):
        exchange(1, piece).start()
        exchange(3, piece).start()
    for piece in range(chunks):
        @pl.when((x == 0) | ((x == 1) & (piece < EARLY)))
        def _():
            forward_own(piece).start()

    @pl.when(x == 2)
    def _():
        forward_last(0, 0, True).start()

    def send_near(step):
        return remote(
            sums.at[x_at[step]], near.at[NX - step - 1], ns_sem.at[step - 1], nr_sem.at[NX - step - 1], x_peer(step)
        )

    def send_far(step):
        return remote(partial, far.at[NG - step - 1], fs_sem.at[step - 1], fr_sem.at[NG - step - 1], g_peer(step))

    def one_hop(piece):
        arrival(3, piece).wait_recv()
        arrival(1, piece).wait_recv()

        @pl.when((x == 1) | (x == 2))
        def _():
            forward(x - 1, piece).start()

        @pl.when(x == 3)
        def _():
            forward(0, piece).start()

        if (piece + 1) * CHUNK == band:
            @pl.when(x == 3)
            def _():
                forward_last(0, 0).start()
        if piece + WINDOW < chunks:
            exchange(1, piece + WINDOW).start()
            exchange(3, piece + WINDOW).start()
        else:
            some = chunks // WINDOW
            for late in range(some):
                exchange(2, (piece + WINDOW - chunks) * some + late).start()

    sums[...] = jnp.zeros_like(sums)
    ones = jnp.ones((8, hours), BF16)
    for q in range(NX):
        stage[q].wait()
        for piece in range(quarter // 512):
            some = lax.dot_general(
                ones, weighted[q, pl.ds(piece * 512, 512)], CROSS_LANES, preferred_element_type=F32
            )
            for part in range(4):
                sums[q, pl.ds(piece * 4 + part, 1)] = some[0:1, part * LANES : (part + 1) * LANES]
        if q:
            one_hop(q - 1)
    keep.wait()
    for step in range(1, NX):
        send_near(step).start()

    live = count[0]
    groups = listed.shape[0]

    def mark(part, mask):
        value = listed[pl.ds(part, 1), :]
        high = jnp.broadcast_to(value // LANES, (groups, LANES))
        low = jnp.broadcast_to(value % LANES, (LANES, LANES))
        place = lax.broadcasted_iota(jnp.int32, (LANES, LANES), 1) + part * LANES
        left = jnp.where(high == lax.broadcasted_iota(jnp.int32, (groups, LANES), 0), 1.0, 0.0).astype(BF16)
        hit = (low == lax.broadcasted_iota(jnp.int32, (LANES, LANES), 0)) & (place < live)
        right = jnp.where(hit, 1.0, 0.0).astype(BF16)
        return mask + lax.dot_general(left, right, CROSS_LANES, preferred_element_type=F32)

    mask = jnp.zeros((groups, LANES), F32)
    for q in range(4):
        mask = lax.fori_loop(q * (groups // 4), (q + 1) * (groups // 4), mark, mask)
        one_hop(3 + q)
    scale[...] = mask * area[...]

    def spread(row_of, target):
        for a in range(tiles):
            target[pl.ds(a * LANES, LANES)] = jnp.broadcast_to(row_of(a), (LANES, LANES)).T

    for step in range(1, NX):
        send_near(step).wait_recv()
    partial[...] = sums[x] + near[0] + near[1] + near[2]
    for step in range(1, NG):
        send_far(step).start()
    one_hop(7)
    spread(lambda a: scale[pl.ds(x * tiles + a, 1)], scales)
    for piece in range(8, chunks):
        one_hop(piece)

    for piece in range(chunks):
        @pl.when(x == 0)
        def _():
            forward(1, piece).start()
        if piece >= EARLY:
            @pl.when(x == 1)
            def _():
                forward_own(piece).start()

    for step in range(1, NG):
        send_far(step).wait_recv()
    total = partial[...]
    for step in range(NG - 1):
        total = total + far[step]
    mean = total[:tiles] / (hours * NX * NG)
    spread(lambda a: mean[a : a + 1], means)

    def weigh(source, target, piece, first=0, size=None):
        r = rows_of(piece)
        m, s = means[r], scales[r]
        for lane in range(first, first + (size or hours), LANES):
            at = pl.ds(lane, LANES)
            target[r, at] = ((source[r, at].astype(F32) - m) * s).astype(BF16)

    def pick(values):
        at = x if len(values) == NX else zh * NX + x
        value = values[0]
        for n in range(1, len(values)):
            value = jnp.where(at == n, values[n], value)
        return value

    def lag_pair(pairs):
        return pick([i for i, _ in pairs]), pick([k for _, k in pairs])

    def slot_of(i, k):
        return i * 2 + k // 2

    def part_of(part):
        return pl.ds(part * half, half)

    def swap(slot, part):
        return remote(
            csend.at[slot, part_of(part)], crecv.at[slot, part_of(part)],
            cs_sem.at[slot, part], cr_sem.at[slot, part], partner,
        )

    def to_owner(i, k, part):
        away = lax.rem(x - i + NX, NX)
        at = lax.rem(away + NX - 1, NX)
        slot = slot_of(i, k)
        return remote(
            xsend.at[slot, part_of(part)], xrecv.at[at, k // 2, part_of(part)],
            ps_sem.at[slot, part], pr_sem.at[at, k // 2, part], (row, group * NX + i),
        )

    def multiply(i, k, parts=range(PARTS)):
        slot = slot_of(i, k)
        mine = core == lax.rem(k, 2)
        for part in parts:
            value = lax.dot_general(
                weighted[i + k, :, part * half : (part + 1) * half], weighted[i],
                CROSS_ROWS, preferred_element_type=F32,
            )

            @pl.when(mine)
            def _():
                own[slot, part_of(part)] = value

            @pl.when(jnp.logical_not(mine))
            def _():
                csend[slot, part_of(part)] = value
                swap(slot, part).start()

    def relay(i, k, part):
        slot = slot_of(i, k)
        return remote(
            xsend.at[slot, part_of(part)], between.at[part, k // 2],
            ps_sem.at[slot, part], bs_sem.at[part, k // 2], x_peer(1 if part == 0 else NX - 1),
        )

    def both_cores(slot, part):
        at = part_of(part)
        return own[slot, at] + crecv[slot, at]

    def finish(i, k):
        slot = slot_of(i, k)
        away = lax.rem(i - x + NX, NX)

        @pl.when(core == lax.rem(k, 2))
        def _():
            for part in range(PARTS):
                at = part_of(part)
                swap(slot, part).wait_recv()
                straight = 3 if part == 0 else 1

                @pl.when((away == straight) | (away == 2))
                def _():
                    xsend[slot, at] = both_cores(slot, part).astype(BF16)

                @pl.when(away == straight)
                def _():
                    to_owner(i, k, part).start()

                @pl.when(away == 2)
                def _():
                    relay(i, k, part).start()

                @pl.when((away == 0) | (away == NX - straight))
                def _():
                    own[slot, at] = both_cores(slot, part)

    def pass_sum(part, kk):
        i = x_at[1 if part == 0 else NX - 1]
        k = kk * 2 + core
        slot = slot_of(i, k)
        at = part_of(part)

        @pl.when((i != LAST_PAIR[0]) | (k != LAST_PAIR[1]))
        def _():
            relay(i, k, part).wait_recv()
            xsend[slot, at] = (own[slot, at] + between[part, kk].astype(F32)).astype(BF16)
            to_owner(i, k, part).start()

    def finish_last(part):
        i, k = LAST_PAIR
        slot = slot_of(i, k)
        at = part_of(part)

        @pl.when(core == k % 2)
        def _():
            swap(slot, part).wait_recv()

            @pl.when(x == i)
            def _():
                own[slot, at] = both_cores(slot, part)

            @pl.when(x != i)
            def _():
                xsend[slot, at] = both_cores(slot, part).astype(BF16)
                to_owner(i, k, part).start()

    for piece in range(chunks):
        for step in (0, 1, 3):
            weigh(raw.at[x_at[step]], weighted.at[x_at[step]], piece)
    def take_halo(block, piece):
        forward(block, piece).wait_recv()
        weigh(weighted.at[NX + block], weighted.at[NX + block], piece)

    ahead = jnp.where(x == 2, 1, 0)
    near_pairs = [lag_pair(pairs) for pairs in NEAR_PAIRS]
    next_pairs = [lag_pair(pairs) for pairs in NEXT_PAIRS]
    for piece in range(chunks):
        arrival(2, piece).wait_recv()

        @pl.when((x == 2) | (x == 3))
        def _():
            forward(x_at[2], piece).start()
        weigh(raw.at[x_at[2]], weighted.at[x_at[2]], piece)
        if piece < len(near_pairs):
            multiply(*near_pairs[piece])
        elif piece < chunks - 2:
            for more in range(3):
                take_halo(ahead, (piece - len(near_pairs)) * 3 + more)
        else:
            multiply(*next_pairs[piece - chunks + 2])
    for part in range(PARTS):
        for at in range(BANDS):
            if part or at:
                @pl.when(x == 2)
                def _():
                    forward_last(part, at, True).start()

                @pl.when(x != 2)
                def _():
                    forward_last(part, at).start()
            else:
                @pl.when(x < 2)
                def _():
                    forward_last(part, at).start()

    out_pairs = [lag_pair(pairs) for pairs in OUT_PAIRS]
    sent = 0
    for upto, pairs in zip(OUT_AT, (FAR_ORDER, THEN_ORDER, [])):
        for pair in out_pairs[sent:upto]:
            finish(*pair)
        sent = upto
        if pairs is THEN_ORDER:
            for piece in range(chunks):
                take_halo(1 - ahead, piece)
        for each in pairs:
            multiply(*lag_pair(each))
    for kk in (1 - zh, zh):
        for part in range(PARTS):
            pass_sum(part, kk)

    def gathered(kk, part):
        def came(d):
            return remote(
                xsend.at[0, part_of(part)], xrecv.at[d, kk, part_of(part)],
                ps_sem.at[0, part], pr_sem.at[d, kk, part], x_peer(d + 1),
            )

        @pl.when((x == LAST_PAIR[0]) & (kk * 2 + core == LAST_PAIR[1]))
        def _():
            came(1).wait_recv()
            slot, at = slot_of(*LAST_PAIR), part_of(part)
            own[slot, at] = own[slot, at] + xrecv[1, LAST_PAIR[1] // 2, at].astype(F32)
        value = own[x * 2 + kk, part_of(part)]
        for d in (0, 2):
            came(d).wait_recv()
            value = value + xrecv[d, kk, part_of(part)].astype(F32)
        return value

    def across(part):
        return remote(
            zsend.at[part_of(part)], zrecv.at[part_of(part)], zs_sem.at[part], zr_sem.at[part], opposite
        )

    def send_across():
        for part in range(PARTS):
            zsend[part_of(part)] = gathered(1 - zh, part).astype(BF16)
            across(part).start()

    last = (x == NX - 1) & (core == 1) & (zh == 0)
    for part in range(PARTS):
        for at in range(BANDS):
            forward_last(part, at).wait_recv()
            for piece in range(at * band // CHUNK, (at + 1) * band // CHUNK):
                weigh(weighted.at[NX + 2], weighted.at[NX + 2], piece, part * half, half)
        multiply(*LAST_PAIR, [part])
        if not part:
            @pl.when(jnp.logical_not(last))
            def _():
                send_across()
        finish_last(part)

    @pl.when(last)
    def _():
        send_across()
    for part in range(PARTS):
        value = gathered(zh, part)
        across(part).wait_recv()
        out[part_of(part)] = (value + zrecv[part_of(part)].astype(F32)) / math.sqrt(quarter * NX * 4)

    for step in range(1, NX):
        for piece in range(chunks):
            exchange(step, piece).wait_send()
        send_near(step).wait_send()
    for step in range(1, NG):
        send_far(step).wait_send()
    for block in range(NX - 2):
        for piece in range(chunks):
            forward(block, piece).wait_send()
    for part in range(PARTS):
        for at in range(BANDS):
            forward_last(part, at).wait_send()
    for i in range(NX):
        for k in range(LAGS):
            for part in range(PARTS):
                @pl.when(core != k % 2)
                def _():
                    swap(slot_of(i, k), part).wait_send()

                @pl.when((core == k % 2) & (x != i))
                def _():
                    to_owner(i, k, part).wait_send()
    for part in range(PARTS):
        across(part).wait_send()


def body(temps, area, ocean_rows, counts):
    rows, hours = temps.shape
    quarter = rows // NX
    chunks = quarter // CHUNK
    vmem = pl.BlockSpec(memory_space=pltpu.VMEM)
    dma = pltpu.SemaphoreType.DMA
    return pl.pallas_call(
        kernel,
        out_shape=jax.ShapeDtypeStruct((hours, hours), F32),
        in_specs=[
            pl.BlockSpec(memory_space=pl.ANY), vmem, vmem, pl.BlockSpec(memory_space=pltpu.SMEM),
        ],
        out_specs=vmem,
        scratch_shapes=[
            pltpu.VMEM((NX, quarter, hours), BF16),
            pltpu.VMEM((2 * NX - 1, quarter, hours), BF16),
            pltpu.VMEM((2 * NX, hours, hours), F32),
            pltpu.VMEM((2 * NX, hours, hours), F32),
            pltpu.VMEM((2 * NX, hours, hours), F32),
            pltpu.VMEM((2 * NX, hours, hours), BF16),
            pltpu.VMEM((NX - 1, 2, hours, hours), BF16),
            pltpu.VMEM((PARTS, 2, hours // PARTS, hours), BF16),
            pltpu.VMEM((hours, hours), BF16),
            pltpu.VMEM((hours, hours), BF16),
            pltpu.VMEM((NX, 16, LANES), F32),
            pltpu.VMEM((NX - 1, 16, LANES), F32),
            pltpu.VMEM((16, LANES), F32),
            pltpu.VMEM((NG - 1, 16, LANES), F32),
            pltpu.VMEM((rows // LANES, LANES), F32),
            pltpu.VMEM((quarter, LANES), F32),
            pltpu.VMEM((quarter, LANES), F32),
            dma((NX + 1,)),
            dma((NX - 1, chunks)), dma((NX - 1, chunks)),
            dma((NX - 2, chunks)), dma((NX - 2, chunks)),
            dma((PARTS, BANDS)), dma((PARTS, BANDS)),
            dma((2 * NX, PARTS)), dma((2 * NX, PARTS)),
            dma((2 * NX, PARTS)), dma((NX - 1, 2, PARTS)), dma((PARTS, 2)),
            dma((PARTS,)), dma((PARTS,)),
            dma((NX - 1,)), dma((NX - 1,)),
            dma((NG - 1,)), dma((NG - 1,)),
        ],
        compiler_params=pltpu.CompilerParams(
            collective_id=0, has_side_effects=True, vmem_limit_bytes=62 << 20
        ),
        cost_estimate=pl.CostEstimate(
            flops=2 * LAGS * hours * hours * rows, bytes_accessed=2 * rows * hours, transcendentals=0
        ),
        name="lagged_band",
    )(temps, area.reshape(-1, LANES), ocean_rows.reshape(-1, LANES), counts)


def solution(mesh):
    in_specs = (P("row", "tm"), P("row"), P("row"), P("row"))
    out_specs = P("row", "tm")
    return jax.shard_map(body, mesh=mesh, in_specs=in_specs, out_specs=out_specs, check_vma=False)
```

```python
import functools
import math

import jax
import jax.numpy as jnp
from jax import lax
from jax.experimental import pallas as pl
from jax.experimental.pallas import tpu as pltpu
from jax.sharding import PartitionSpec as P

LAGS = 4
NX = 4
NG = 8
LANES = 128
CHUNK = 128
EARLY = 2
WINDOW = 6
BANDS = 3
LAST_PARTS = 4
MESH = pl.DeviceIdType.MESH
F32 = jnp.float32
BF16 = jnp.bfloat16
CROSS_ROWS = (((0,), (0,)), ((), ()))
CROSS_LANES = (((1,), (1,)), ((), ()))
PARTS = 2


NEAR_PAIRS = list(zip(
    [(1, 0), (3, 0), (1, 2), (0, 0), (0, 1), (0, 3)],
    [(0, 0), (2, 0), (0, 1), (0, 2), (1, 0), (1, 1)],
    [(1, 0), (3, 0), (1, 1), (1, 2), (2, 0), (2, 1)],
    [(0, 0), (2, 0), (0, 2), (2, 1), (0, 3), (3, 0)],
))
NEXT_PAIRS = list(zip(
    [(3, 1), (1, 3)],
    [(2, 2), (1, 3)],
    [(3, 2), (2, 3)],
    [(2, 2), (3, 1)],
))
FAR_PAIRS = list(zip(
    [(2, 0), (2, 1), (1, 1), (0, 2)],
    [(3, 0), (2, 1), (0, 3), (1, 2)],
    [(0, 0), (0, 1), (0, 2), (0, 3)],
    [(1, 0), (1, 1), (0, 1), (1, 2)],
))
THEN_PAIRS = list(zip(
    [(2, 2), (3, 2), (2, 3)],
    [(3, 1), (2, 3), (3, 2)],
    [(1, 3), (3, 1), (2, 2)],
    [(1, 3), (2, 3), (3, 2)],
))
LAST_PAIR = (3, 3)
OUT_AT = (5, 12, 15)


def crossing_first(pairs, zh):
    return sorted(pairs, key=lambda pair: pair[1] // 2 == zh)


def out_order(zh, x):
    def best(pool, taken):
        def rank(pair):
            i, k = pair
            since = [n for n, (owner, _) in enumerate(taken) if owner == i]
            return (i == x, k // 2 == zh, since[-1] if since else -1, pool.index(pair))

        return min(pool, key=rank)

    pool = [pairs[x] for pairs in NEAR_PAIRS + NEXT_PAIRS]
    taken = []
    for upto, more in zip(OUT_AT, (FAR_PAIRS, THEN_PAIRS, [])):
        while len(taken) < upto:
            pair = best(pool, taken)
            pool.remove(pair)
            taken.append(pair)
        pool += [pairs[x] for pairs in more]
    return taken


def by_place(order):
    return list(zip(*[order(zh, x) for zh in range(2) for x in range(NX)]))


OUT_PAIRS = by_place(out_order)
FAR_ORDER = by_place(lambda zh, x: crossing_first([pairs[x] for pairs in FAR_PAIRS], zh))
THEN_ORDER = by_place(lambda zh, x: crossing_first([pairs[x] for pairs in THEN_PAIRS], zh))


def kernel(
    temps, area, listed, count, out,
    raw, weighted, own, csend, crecv, xsend, xrecv, between, zsend, zrecv,
    sums, near, partial, far, scale, means, scales, local_sem,
    xs_sem, xr_sem, hs_sem, hr_sem, ls_sem, lr_sem, cs_sem, cr_sem, ps_sem, pr_sem, bs_sem, zs_sem, zr_sem,
    ns_sem, nr_sem, fs_sem, fr_sem,
    lcs_sem, lcr_sem, lps_sem, lpr_sem, lzs_sem, lzr_sem,
):
    row, tm = lax.axis_index("row"), lax.axis_index("tm")
    zh, core = row // 2, lax.rem(row, 2)
    group, x = tm // NX, lax.rem(tm, NX)
    quarter = raw.shape[1]
    chunks = quarter // CHUNK
    tiles = quarter // LANES
    hours = raw.shape[2]
    half = hours // PARTS

    def x_peer(step):
        return (row, group * NX + lax.rem(x + step, NX))

    def g_peer(step):
        return (row, lax.rem(group + step, NG) * NX + x)

    partner = (zh * 2 + 1 - core, tm)
    opposite = (lax.rem(row + 2, 4), tm)
    x_at = [lax.rem(x + step, NX) for step in range(NX)]

    barrier = pltpu.get_barrier_semaphore()
    everyone = [x_peer(s) for s in range(1, NX)] + [g_peer(s) for s in range(1, NG)]
    everyone += [partner, opposite]
    for device in everyone:
        pl.semaphore_signal(barrier, inc=1, device_id=device, device_id_type=MESH)

    def remote(src, dst, send, recv, device):
        return pltpu.make_async_remote_copy(
            src_ref=src, dst_ref=dst, send_sem=send, recv_sem=recv, device_id=device, device_id_type=MESH
        )

    def rows_of(piece, base=0):
        return pl.ds(pl.multiple_of(base + piece * CHUNK, CHUNK), CHUNK)

    stage = [
        pltpu.make_async_copy(
            temps.at[pl.ds(q * quarter, quarter)], weighted.at[q], local_sem.at[q]
        )
        for q in range(NX)
    ]
    keep = pltpu.make_async_copy(
        temps.at[pl.ds(pl.multiple_of(x * quarter, quarter), quarter)], raw.at[x], local_sem.at[NX]
    )
    for copy in stage:
        copy.start()
    keep.start()

    def exchange(step, piece):
        target = x_at[step]
        return remote(
            temps.at[rows_of(piece, target * quarter)], raw.at[x, rows_of(piece)],
            xs_sem.at[step - 1, piece], xr_sem.at[NX - step - 1, piece], x_peer(step),
        )

    def arrival(step, piece):
        source = x_at[step]
        return remote(
            temps.at[rows_of(piece)], raw.at[source, rows_of(piece)],
            xs_sem.at[0, 0], xr_sem.at[step - 1, piece], x_peer(step),
        )

    def forward(block, piece):
        return remote(
            raw.at[block, rows_of(piece)], weighted.at[NX + block, rows_of(piece)],
            hs_sem.at[block, piece], hr_sem.at[block, piece], g_peer(NG - 1),
        )

    def forward_own(piece):
        return remote(
            temps.at[rows_of(piece, x * quarter)], weighted.at[NX + x, rows_of(piece)],
            hs_sem.at[x, piece], hr_sem.at[x, piece], g_peer(NG - 1),
        )

    band = quarter // BANDS
    thin = hours // LAST_PARTS

    def last_part(part):
        return pl.ds(part * thin, thin)

    def forward_last(part, at, mine=False):
        r, cols = pl.ds(at * band, band), last_part(part)
        source = raw.at[2, r, cols]
        if mine:
            source = temps.at[pl.ds(pl.multiple_of(x * quarter + at * band, band), band), cols]
        return remote(
            source, weighted.at[NX + 2, r, cols], ls_sem.at[part, at], lr_sem.at[part, at], g_peer(NG - 1)
        )

    pl.semaphore_wait(barrier, len(everyone))

    for piece in range(WINDOW):
        exchange(1, piece).start()
        exchange(3, piece).start()
    for piece in range(chunks):
        @pl.when((x == 0) | ((x == 1) & (piece < EARLY)))
        def _():
            forward_own(piece).start()

    @pl.when(x == 2)
    def _():
        forward_last(0, 0, True).start()

    def send_near(step):
        return remote(
            sums.at[x_at[step]], near.at[NX - step - 1], ns_sem.at[step - 1], nr_sem.at[NX - step - 1], x_peer(step)
        )

    def send_far(step):
        return remote(partial, far.at[NG - step - 1], fs_sem.at[step - 1], fr_sem.at[NG - step - 1], g_peer(step))

    def one_hop(piece):
        arrival(3, piece).wait_recv()
        arrival(1, piece).wait_recv()

        @pl.when((x == 1) | (x == 2))
        def _():
            forward(x - 1, piece).start()

        @pl.when(x == 3)
        def _():
            forward(0, piece).start()

        if (piece + 1) * CHUNK == band:
            @pl.when(x == 3)
            def _():
                forward_last(0, 0).start()
        if piece + WINDOW < chunks:
            exchange(1, piece + WINDOW).start()
            exchange(3, piece + WINDOW).start()
        else:
            some = chunks // WINDOW
            for late in range(some):
                exchange(2, (piece + WINDOW - chunks) * some + late).start()

    sums[...] = jnp.zeros_like(sums)
    ones = jnp.ones((8, hours), BF16)
    for q in range(NX):
        stage[q].wait()
        for piece in range(quarter // 512):
            some = lax.dot_general(
                ones, weighted[q, pl.ds(piece * 512, 512)], CROSS_LANES, preferred_element_type=F32
            )
            for part in range(4):
                sums[q, pl.ds(piece * 4 + part, 1)] = some[0:1, part * LANES : (part + 1) * LANES]
        if q < 3:
            one_hop(q)
    keep.wait()
    for step in range(1, NX):
        send_near(step).start()

    live = count[0]
    groups = listed.shape[0]

    def mark(part, mask):
        value = listed[pl.ds(part, 1), :]
        high = jnp.broadcast_to(value // LANES, (groups, LANES))
        low = jnp.broadcast_to(value % LANES, (LANES, LANES))
        place = lax.broadcasted_iota(jnp.int32, (LANES, LANES), 1) + part * LANES
        left = jnp.where(high == lax.broadcasted_iota(jnp.int32, (groups, LANES), 0), 1.0, 0.0).astype(BF16)
        hit = (low == lax.broadcasted_iota(jnp.int32, (LANES, LANES), 0)) & (place < live)
        right = jnp.where(hit, 1.0, 0.0).astype(BF16)
        return mask + lax.dot_general(left, right, CROSS_LANES, preferred_element_type=F32)

    mask = jnp.zeros((groups, LANES), F32)
    for q in range(4):
        mask = lax.fori_loop(q * (groups // 4), (q + 1) * (groups // 4), mark, mask)
        one_hop(3 + q)
    scale[...] = mask * area[...]

    def spread(row_of, target):
        for a in range(tiles):
            target[pl.ds(a * LANES, LANES)] = jnp.broadcast_to(row_of(a), (LANES, LANES)).T

    for step in range(1, NX):
        send_near(step).wait_recv()
    partial[...] = sums[x] + near[0] + near[1] + near[2]
    for step in range(1, NG):
        send_far(step).start()
    one_hop(7)
    spread(lambda a: scale[pl.ds(x * tiles + a, 1)], scales)
    for piece in range(8, chunks):
        one_hop(piece)

    for piece in range(chunks):
        @pl.when(x == 0)
        def _():
            forward(1, piece).start()
        if piece >= EARLY:
            @pl.when(x == 1)
            def _():
                forward_own(piece).start()

    for step in range(1, NG):
        send_far(step).wait_recv()
    total = partial[...]
    for step in range(NG - 1):
        total = total + far[step]
    mean = total[:tiles] / (hours * NX * NG)
    spread(lambda a: mean[a : a + 1], means)

    def weigh(source, target, piece, first=0, size=None):
        r = rows_of(piece)
        m, s = means[r], scales[r]
        for lane in range(first, first + (size or hours), LANES):
            at = pl.ds(lane, LANES)
            target[r, at] = ((source[r, at].astype(F32) - m) * s).astype(BF16)

    def pick(values):
        at = x if len(values) == NX else zh * NX + x
        value = values[0]
        for n in range(1, len(values)):
            value = jnp.where(at == n, values[n], value)
        return value

    def lag_pair(pairs):
        return pick([i for i, _ in pairs]), pick([k for _, k in pairs])

    def slot_of(i, k):
        return i * 2 + k // 2

    def part_of(part):
        return pl.ds(part * half, half)

    def swap(slot, part):
        return remote(
            csend.at[slot, part_of(part)], crecv.at[slot, part_of(part)],
            cs_sem.at[slot, part], cr_sem.at[slot, part], partner,
        )

    def to_owner(i, k, part):
        away = lax.rem(x - i + NX, NX)
        at = lax.rem(away + NX - 1, NX)
        slot = slot_of(i, k)
        return remote(
            xsend.at[slot, part_of(part)], xrecv.at[at, k // 2, part_of(part)],
            ps_sem.at[slot, part], pr_sem.at[at, k // 2, part], (row, group * NX + i),
        )

    def multiply(i, k):
        slot = slot_of(i, k)
        mine = core == lax.rem(k, 2)
        for part in range(PARTS):
            value = lax.dot_general(
                weighted[i + k, :, part * half : (part + 1) * half], weighted[i],
                CROSS_ROWS, preferred_element_type=F32,
            )

            @pl.when(mine)
            def _():
                own[slot, part_of(part)] = value

            @pl.when(jnp.logical_not(mine))
            def _():
                csend[slot, part_of(part)] = value
                swap(slot, part).start()

    def relay(i, k, part):
        slot = slot_of(i, k)
        return remote(
            xsend.at[slot, part_of(part)], between.at[part, k // 2],
            ps_sem.at[slot, part], bs_sem.at[part, k // 2], x_peer(1 if part == 0 else NX - 1),
        )

    def both_cores(slot, part):
        at = part_of(part)
        return own[slot, at] + crecv[slot, at]

    def finish(i, k):
        slot = slot_of(i, k)
        away = lax.rem(i - x + NX, NX)

        @pl.when(core == lax.rem(k, 2))
        def _():
            for part in range(PARTS):
                at = part_of(part)
                swap(slot, part).wait_recv()
                straight = 3 if part == 0 else 1

                @pl.when((away == straight) | (away == 2))
                def _():
                    xsend[slot, at] = both_cores(slot, part).astype(BF16)

                @pl.when(away == straight)
                def _():
                    to_owner(i, k, part).start()

                @pl.when(away == 2)
                def _():
                    relay(i, k, part).start()

                @pl.when((away == 0) | (away == NX - straight))
                def _():
                    own[slot, at] = both_cores(slot, part)

    def pass_sum(part, kk):
        i = x_at[1 if part == 0 else NX - 1]
        k = kk * 2 + core
        slot = slot_of(i, k)
        at = part_of(part)

        @pl.when((i != LAST_PAIR[0]) | (k != LAST_PAIR[1]))
        def _():
            relay(i, k, part).wait_recv()
            xsend[slot, at] = (own[slot, at] + between[part, kk].astype(F32)).astype(BF16)
            to_owner(i, k, part).start()

    last_slot, last_kk = slot_of(*LAST_PAIR), LAST_PAIR[1] // 2
    last_mine = core == LAST_PAIR[1] % 2

    def swap_last(part):
        at = last_part(part)
        return remote(csend.at[last_slot, at], crecv.at[last_slot, at], lcs_sem.at[part], lcr_sem.at[part], partner)

    def last_to_owner(part):
        away = lax.rem(x - LAST_PAIR[0] + NX, NX)
        place = lax.rem(away + NX - 1, NX)
        at = last_part(part)
        return remote(
            xsend.at[last_slot, at], xrecv.at[place, last_kk, at],
            lps_sem.at[part], lpr_sem.at[place, part], (row, group * NX + LAST_PAIR[0]),
        )

    def multiply_last(part):
        i, k = LAST_PAIR
        at = last_part(part)
        value = lax.dot_general(
            weighted[i + k, :, part * thin : (part + 1) * thin], weighted[i],
            CROSS_ROWS, preferred_element_type=F32,
        )

        @pl.when(last_mine)
        def _():
            own[last_slot, at] = value

        @pl.when(jnp.logical_not(last_mine))
        def _():
            csend[last_slot, at] = value
            swap_last(part).start()

    def finish_last(part):
        at = last_part(part)

        @pl.when(last_mine)
        def _():
            swap_last(part).wait_recv()
            value = own[last_slot, at] + crecv[last_slot, at]

            @pl.when(x == LAST_PAIR[0])
            def _():
                own[last_slot, at] = value

            @pl.when(x != LAST_PAIR[0])
            def _():
                xsend[last_slot, at] = value.astype(BF16)
                last_to_owner(part).start()

    def gathered_last(part):
        at = last_part(part)
        value = own[last_slot, at]
        for d in range(NX - 1):
            remote(
                xsend.at[last_slot, at], xrecv.at[d, last_kk, at], lps_sem.at[part], lpr_sem.at[d, part], x_peer(d + 1)
            ).wait_recv()
            value = value + xrecv[d, last_kk, at].astype(F32)
        return value

    def across_last(part):
        at = last_part(part)
        return remote(zsend.at[at], zrecv.at[at], lzs_sem.at[part], lzr_sem.at[part], opposite)

    for piece in range(chunks):
        for step in (0, 1, 3):
            weigh(raw.at[x_at[step]], weighted.at[x_at[step]], piece)
    def take_halo(block, piece):
        forward(block, piece).wait_recv()
        weigh(weighted.at[NX + block], weighted.at[NX + block], piece)

    ahead = jnp.where(x == 2, 1, 0)
    near_pairs = [lag_pair(pairs) for pairs in NEAR_PAIRS]
    next_pairs = [lag_pair(pairs) for pairs in NEXT_PAIRS]
    for piece in range(chunks):
        arrival(2, piece).wait_recv()

        @pl.when((x == 2) | (x == 3))
        def _():
            forward(x_at[2], piece).start()
        weigh(raw.at[x_at[2]], weighted.at[x_at[2]], piece)
        if piece < len(near_pairs):
            multiply(*near_pairs[piece])
        elif piece < chunks - 2:
            for more in range(3):
                take_halo(ahead, (piece - len(near_pairs)) * 3 + more)
        else:
            multiply(*next_pairs[piece - chunks + 2])
    for part in range(LAST_PARTS):
        for at in range(BANDS):
            if part or at:
                @pl.when(x == 2)
                def _():
                    forward_last(part, at, True).start()

                @pl.when(x != 2)
                def _():
                    forward_last(part, at).start()
            else:
                @pl.when(x < 2)
                def _():
                    forward_last(part, at).start()

    out_pairs = [lag_pair(pairs) for pairs in OUT_PAIRS]
    sent = 0
    for upto, pairs in zip(OUT_AT, (FAR_ORDER, THEN_ORDER, [])):
        for pair in out_pairs[sent:upto]:
            finish(*pair)
        sent = upto
        if pairs is THEN_ORDER:
            for piece in range(chunks):
                take_halo(1 - ahead, piece)
        for each in pairs:
            multiply(*lag_pair(each))
    for kk in (1 - zh, zh):
        for part in range(PARTS):
            pass_sum(part, kk)

    def gathered(kk, part):
        def came(d):
            return remote(
                xsend.at[0, part_of(part)], xrecv.at[d, kk, part_of(part)],
                ps_sem.at[0, part], pr_sem.at[d, kk, part], x_peer(d + 1),
            )

        value = own[x * 2 + kk, part_of(part)]
        for d in (0, 2):
            came(d).wait_recv()
            value = value + xrecv[d, kk, part_of(part)].astype(F32)
        return value

    def across(part):
        return remote(
            zsend.at[part_of(part)], zrecv.at[part_of(part)], zs_sem.at[part], zr_sem.at[part], opposite
        )

    def send_across():
        for part in range(PARTS):
            zsend[part_of(part)] = gathered(1 - zh, part).astype(BF16)
            across(part).start()

    owner = (x == LAST_PAIR[0]) & last_mine & (zh == last_kk)
    sender = (x == LAST_PAIR[0]) & last_mine & (zh != last_kk)
    for part in range(LAST_PARTS):
        for at in range(BANDS):
            forward_last(part, at).wait_recv()
            for piece in range(at * band // CHUNK, (at + 1) * band // CHUNK):
                weigh(weighted.at[NX + 2], weighted.at[NX + 2], piece, part * thin, thin)
        multiply_last(part)
        if part == 1:
            @pl.when(jnp.logical_not(sender))
            def _():
                send_across()
        if part:
            finish_last(part - 1)
    finish_last(LAST_PARTS - 1)

    @pl.when(sender)
    def _():
        for part in range(LAST_PARTS):
            zsend[last_part(part)] = gathered_last(part).astype(BF16)
            across_last(part).start()

    divisor = math.sqrt(quarter * NX * 4)

    @pl.when(owner)
    def _():
        for part in range(LAST_PARTS):
            at = last_part(part)
            value = gathered_last(part)
            across_last(part).wait_recv()
            out[at] = (value + zrecv[at].astype(F32)) / divisor

    @pl.when(jnp.logical_not(owner))
    def _():
        for part in range(PARTS):
            at = part_of(part)
            value = gathered(zh, part)
            across(part).wait_recv()
            out[at] = (value + zrecv[at].astype(F32)) / divisor

    for step in range(1, NX):
        for piece in range(chunks):
            exchange(step, piece).wait_send()
        send_near(step).wait_send()
    for step in range(1, NG):
        send_far(step).wait_send()
    for block in range(NX - 2):
        for piece in range(chunks):
            forward(block, piece).wait_send()
    for part in range(LAST_PARTS):
        for at in range(BANDS):
            forward_last(part, at).wait_send()
    for i in range(NX):
        for k in range(LAGS):
            if (i, k) == LAST_PAIR:
                continue
            for part in range(PARTS):
                @pl.when(core != k % 2)
                def _():
                    swap(slot_of(i, k), part).wait_send()

                @pl.when((core == k % 2) & (x != i))
                def _():
                    to_owner(i, k, part).wait_send()
    for part in range(LAST_PARTS):
        @pl.when(jnp.logical_not(last_mine))
        def _():
            swap_last(part).wait_send()

        @pl.when(last_mine & (x != LAST_PAIR[0]))
        def _():
            last_to_owner(part).wait_send()

        @pl.when(sender)
        def _():
            across_last(part).wait_send()
    for part in range(PARTS):
        @pl.when(jnp.logical_not(sender))
        def _():
            across(part).wait_send()


def body(temps, area, ocean_rows, counts):
    rows, hours = temps.shape
    quarter = rows // NX
    chunks = quarter // CHUNK
    vmem = pl.BlockSpec(memory_space=pltpu.VMEM)
    dma = pltpu.SemaphoreType.DMA
    return pl.pallas_call(
        kernel,
        out_shape=pltpu.VMEM((hours, hours), F32),
        in_specs=[
            pl.BlockSpec(memory_space=pl.ANY), vmem, vmem, pl.BlockSpec(memory_space=pltpu.SMEM),
        ],
        out_specs=vmem,
        scratch_shapes=[
            pltpu.VMEM((NX, quarter, hours), BF16),
            pltpu.VMEM((2 * NX - 1, quarter, hours), BF16),
            pltpu.VMEM((2 * NX, hours, hours), F32),
            pltpu.VMEM((2 * NX, hours, hours), F32),
            pltpu.VMEM((2 * NX, hours, hours), F32),
            pltpu.VMEM((2 * NX, hours, hours), BF16),
            pltpu.VMEM((NX - 1, 2, hours, hours), BF16),
            pltpu.VMEM((PARTS, 2, hours // PARTS, hours), BF16),
            pltpu.VMEM((hours, hours), BF16),
            pltpu.VMEM((hours, hours), BF16),
            pltpu.VMEM((NX, 16, LANES), F32),
            pltpu.VMEM((NX - 1, 16, LANES), F32),
            pltpu.VMEM((16, LANES), F32),
            pltpu.VMEM((NG - 1, 16, LANES), F32),
            pltpu.VMEM((rows // LANES, LANES), F32),
            pltpu.VMEM((quarter, LANES), F32),
            pltpu.VMEM((quarter, LANES), F32),
            dma((NX + 1,)),
            dma((NX - 1, chunks)), dma((NX - 1, chunks)),
            dma((NX - 2, chunks)), dma((NX - 2, chunks)),
            dma((LAST_PARTS, BANDS)), dma((LAST_PARTS, BANDS)),
            dma((2 * NX, PARTS)), dma((2 * NX, PARTS)),
            dma((2 * NX, PARTS)), dma((NX - 1, 2, PARTS)), dma((PARTS, 2)),
            dma((PARTS,)), dma((PARTS,)),
            dma((NX - 1,)), dma((NX - 1,)),
            dma((NG - 1,)), dma((NG - 1,)),
            dma((LAST_PARTS,)), dma((LAST_PARTS,)),
            dma((LAST_PARTS,)), dma((NX - 1, LAST_PARTS)),
            dma((LAST_PARTS,)), dma((LAST_PARTS,)),
        ],
        compiler_params=pltpu.CompilerParams(
            collective_id=0, has_side_effects=True, vmem_limit_bytes=56 << 20
        ),
        cost_estimate=pl.CostEstimate(
            flops=2 * LAGS * hours * hours * rows, bytes_accessed=2 * rows * hours, transcendentals=0
        ),
        name="lagged_band",
    )(temps, area.reshape(-1, LANES), ocean_rows.reshape(-1, LANES), counts)


def solution(mesh):
    in_specs = (P("row", "tm"), P("row"), P("row"), P("row"))
    out_specs = P("row", "tm")
    return jax.shard_map(body, mesh=mesh, in_specs=in_specs, out_specs=out_specs, check_vma=False)
```

```python
import functools
import math

import jax
import jax.numpy as jnp
from jax import lax
from jax.experimental import pallas as pl
from jax.experimental.pallas import tpu as pltpu
from jax.sharding import PartitionSpec as P

LAGS = 4
NX = 4
NG = 8
LANES = 128
CHUNK = 128
EARLY = 2
WINDOW = 6
BANDS = 3
AHEAD = ((0, 0), (1, 0), (0, 1))
LAST_PARTS = 4
MESH = pl.DeviceIdType.MESH
F32 = jnp.float32
BF16 = jnp.bfloat16
CROSS_ROWS = (((0,), (0,)), ((), ()))
CROSS_LANES = (((1,), (1,)), ((), ()))
PARTS = 2


NEAR_PAIRS = list(zip(
    [(1, 0), (3, 0), (1, 2), (0, 0), (0, 1), (0, 3)],
    [(0, 0), (2, 0), (0, 1), (0, 2), (1, 0), (1, 1)],
    [(1, 0), (3, 0), (1, 1), (1, 2), (2, 0), (2, 1)],
    [(0, 0), (2, 0), (0, 2), (2, 1), (0, 3), (3, 0)],
))
NEXT_PAIRS = list(zip(
    [(3, 1), (1, 3)],
    [(2, 2), (1, 3)],
    [(3, 2), (2, 3)],
    [(2, 2), (3, 1)],
))
FAR_PAIRS = list(zip(
    [(2, 0), (2, 1), (1, 1), (0, 2)],
    [(3, 0), (2, 1), (0, 3), (1, 2)],
    [(0, 0), (0, 1), (0, 2), (0, 3)],
    [(1, 0), (1, 1), (0, 1), (1, 2)],
))
THEN_PAIRS = list(zip(
    [(2, 2), (3, 2), (2, 3)],
    [(3, 1), (2, 3), (3, 2)],
    [(1, 3), (3, 1), (2, 2)],
    [(1, 3), (2, 3), (3, 2)],
))
LAST_PAIR = (3, 3)
OUT_AT = (5, 12, 15)


def crossing_first(pairs, zh):
    return sorted(pairs, key=lambda pair: pair[1] // 2 == zh)


def out_order(zh, x):
    def best(pool, taken):
        def rank(pair):
            i, k = pair
            since = [n for n, (owner, _) in enumerate(taken) if owner == i]
            return (i == x, k // 2 == zh, since[-1] if since else -1, pool.index(pair))

        return min(pool, key=rank)

    pool = [pairs[x] for pairs in NEAR_PAIRS + NEXT_PAIRS]
    taken = []
    for upto, more in zip(OUT_AT, (FAR_PAIRS, THEN_PAIRS, [])):
        while len(taken) < upto:
            pair = best(pool, taken)
            pool.remove(pair)
            taken.append(pair)
        pool += [pairs[x] for pairs in more]
    return taken


def by_place(order):
    return list(zip(*[order(zh, x) for zh in range(2) for x in range(NX)]))


OUT_PAIRS = by_place(out_order)
FAR_ORDER = by_place(lambda zh, x: crossing_first([pairs[x] for pairs in FAR_PAIRS], zh))
THEN_ORDER = by_place(lambda zh, x: crossing_first([pairs[x] for pairs in THEN_PAIRS], zh))


def kernel(
    temps, area_in, listed_in, count, out,
    raw, weighted, own, csend, crecv, xsend, xrecv, between, zsend, zrecv,
    sums, near, partial, far, area, listed, scale, means, scales, local_sem,
    xs_sem, xr_sem, hs_sem, hr_sem, ls_sem, lr_sem, cs_sem, cr_sem, ps_sem, pr_sem, bs_sem, zs_sem, zr_sem,
    ns_sem, nr_sem, fs_sem, fr_sem,
    lcs_sem, lcr_sem, lps_sem, lpr_sem, lzs_sem, lzr_sem,
):
    row, tm = lax.axis_index("row"), lax.axis_index("tm")
    zh, core = row // 2, lax.rem(row, 2)
    group, x = tm // NX, lax.rem(tm, NX)
    quarter = raw.shape[1]
    chunks = quarter // CHUNK
    tiles = quarter // LANES
    hours = raw.shape[2]
    half = hours // PARTS

    def x_peer(step):
        return (row, group * NX + lax.rem(x + step, NX))

    def g_peer(step):
        return (row, lax.rem(group + step, NG) * NX + x)

    partner = (zh * 2 + 1 - core, tm)
    opposite = (lax.rem(row + 2, 4), tm)
    x_at = [lax.rem(x + step, NX) for step in range(NX)]

    barrier = pltpu.get_barrier_semaphore()
    everyone = [x_peer(s) for s in range(1, NX)] + [g_peer(s) for s in range(1, NG)]
    everyone += [partner, opposite]
    for device in everyone:
        pl.semaphore_signal(barrier, inc=1, device_id=device, device_id_type=MESH)

    def remote(src, dst, send, recv, device):
        return pltpu.make_async_remote_copy(
            src_ref=src, dst_ref=dst, send_sem=send, recv_sem=recv, device_id=device, device_id_type=MESH
        )

    def rows_of(piece, base=0):
        return pl.ds(pl.multiple_of(base + piece * CHUNK, CHUNK), CHUNK)

    stage = [
        pltpu.make_async_copy(
            temps.at[pl.ds(q * quarter, quarter)], weighted.at[q], local_sem.at[q]
        )
        for q in range(NX)
    ]
    keep = pltpu.make_async_copy(
        temps.at[pl.ds(pl.multiple_of(x * quarter, quarter), quarter)], raw.at[x], local_sem.at[NX]
    )
    for copy in stage:
        copy.start()
    keep.start()
    tables = [
        pltpu.make_async_copy(area_in, area, local_sem.at[NX + 1]),
        pltpu.make_async_copy(listed_in, listed, local_sem.at[NX + 2]),
    ]
    for copy in tables:
        copy.start()

    def exchange(step, piece):
        target = x_at[step]
        return remote(
            temps.at[rows_of(piece, target * quarter)], raw.at[x, rows_of(piece)],
            xs_sem.at[step - 1, piece], xr_sem.at[NX - step - 1, piece], x_peer(step),
        )

    def arrival(step, piece):
        source = x_at[step]
        return remote(
            temps.at[rows_of(piece)], raw.at[source, rows_of(piece)],
            xs_sem.at[0, 0], xr_sem.at[step - 1, piece], x_peer(step),
        )

    def forward(block, piece):
        return remote(
            raw.at[block, rows_of(piece)], weighted.at[NX + block, rows_of(piece)],
            hs_sem.at[block, piece], hr_sem.at[block, piece], g_peer(NG - 1),
        )

    def forward_own(piece):
        return remote(
            temps.at[rows_of(piece, x * quarter)], weighted.at[NX + x, rows_of(piece)],
            hs_sem.at[x, piece], hr_sem.at[x, piece], g_peer(NG - 1),
        )

    band = quarter // BANDS
    thin = hours // LAST_PARTS

    def last_part(part):
        return pl.ds(part * thin, thin)

    def forward_last(part, at, mine=False):
        r, cols = pl.ds(at * band, band), last_part(part)
        source = raw.at[2, r, cols]
        if mine:
            source = temps.at[pl.ds(pl.multiple_of(x * quarter + at * band, band), band), cols]
        return remote(
            source, weighted.at[NX + 2, r, cols], ls_sem.at[part, at], lr_sem.at[part, at], g_peer(NG - 1)
        )

    pl.semaphore_wait(barrier, len(everyone))

    for piece in range(WINDOW):
        exchange(3, piece).start()
        exchange(1, piece).start()
        if piece < EARLY:
            @pl.when(x < 2)
            def _():
                forward_own(piece).start()
    for piece in range(EARLY, chunks):
        @pl.when(x == 0)
        def _():
            forward_own(piece).start()

    @pl.when(x == 2)
    def _():
        for part, at in AHEAD:
            forward_last(part, at, True).start()

    def send_near(step):
        return remote(
            sums.at[x_at[step]], near.at[NX - step - 1], ns_sem.at[step - 1], nr_sem.at[NX - step - 1], x_peer(step)
        )

    def send_far(step):
        return remote(partial, far.at[NG - step - 1], fs_sem.at[step - 1], fr_sem.at[NG - step - 1], g_peer(step))

    def one_hop(piece):
        arrival(3, piece).wait_recv()
        arrival(1, piece).wait_recv()

        @pl.when((x == 1) | (x == 2))
        def _():
            forward(x - 1, piece).start()

        @pl.when(x == 3)
        def _():
            forward(0, piece).start()

        for part, at in AHEAD:
            if (piece + 1) * CHUNK == (at + 1) * band:
                @pl.when(x == 3)
                def _():
                    forward_last(part, at).start()
        if piece + WINDOW < chunks:
            exchange(1, piece + WINDOW).start()
            exchange(3, piece + WINDOW).start()
        else:
            some = chunks // WINDOW
            for late in range(some):
                exchange(2, (piece + WINDOW - chunks) * some + late).start()

    one_hop(0)
    one_hop(1)

    sums[...] = jnp.zeros_like(sums)
    ones = jnp.ones((8, hours), BF16)
    for q in range(NX):
        stage[q].wait()
        for piece in range(quarter // 512):
            some = lax.dot_general(
                ones, weighted[q, pl.ds(piece * 512, 512)], CROSS_LANES, preferred_element_type=F32
            )
            for part in range(4):
                sums[q, pl.ds(piece * 4 + part, 1)] = some[0:1, part * LANES : (part + 1) * LANES]
        if q < 3:
            one_hop(q + 2)
    keep.wait()
    for copy in tables:
        copy.wait()
    for step in range(1, NX):
        send_near(step).start()

    live = count[0]
    groups = listed.shape[0]

    def mark(part, mask):
        value = listed[pl.ds(part, 1), :]
        high = jnp.broadcast_to(value // LANES, (groups, LANES))
        low = jnp.broadcast_to(value % LANES, (LANES, LANES))
        place = lax.broadcasted_iota(jnp.int32, (LANES, LANES), 1) + part * LANES
        left = jnp.where(high == lax.broadcasted_iota(jnp.int32, (groups, LANES), 0), 1.0, 0.0).astype(BF16)
        hit = (low == lax.broadcasted_iota(jnp.int32, (LANES, LANES), 0)) & (place < live)
        right = jnp.where(hit, 1.0, 0.0).astype(BF16)
        return mask + lax.dot_general(left, right, CROSS_LANES, preferred_element_type=F32)

    mask = jnp.zeros((groups, LANES), F32)
    for q in range(4):
        mask = lax.fori_loop(q * (groups // 4), (q + 1) * (groups // 4), mark, mask)
        one_hop(5 + q)
    scale[...] = mask * area[...]

    def spread(row_of, target):
        for a in range(tiles):
            target[pl.ds(a * LANES, LANES)] = jnp.broadcast_to(row_of(a), (LANES, LANES)).T

    for step in range(1, NX):
        send_near(step).wait_recv()
    partial[...] = sums[x] + near[0] + near[1] + near[2]
    for step in range(1, NG):
        send_far(step).start()
    one_hop(9)
    spread(lambda a: scale[pl.ds(x * tiles + a, 1)], scales)
    for piece in range(10, chunks):
        one_hop(piece)

    for piece in range(chunks):
        @pl.when(x == 0)
        def _():
            forward(1, piece).start()
        if piece >= EARLY:
            @pl.when(x == 1)
            def _():
                forward_own(piece).start()

    def weigh(source, target, piece, first=0, size=None):
        r = rows_of(piece)
        m, s = means[r], scales[r]
        for lane in range(first, first + (size or hours), LANES):
            at = pl.ds(lane, LANES)
            target[r, at] = ((source[r, at].astype(F32) - m) * s).astype(BF16)

    def pick(values):
        at = x if len(values) == NX else zh * NX + x
        value = values[0]
        for n in range(1, len(values)):
            value = jnp.where(at == n, values[n], value)
        return value

    def lag_pair(pairs):
        return pick([i for i, _ in pairs]), pick([k for _, k in pairs])

    def slot_of(i, k):
        return i * 2 + k // 2

    def part_of(part):
        return pl.ds(part * half, half)

    def swap(slot, part):
        return remote(
            csend.at[slot, part_of(part)], crecv.at[slot, part_of(part)],
            cs_sem.at[slot, part], cr_sem.at[slot, part], partner,
        )

    def to_owner(i, k, part):
        away = lax.rem(x - i + NX, NX)
        at = lax.rem(away + NX - 1, NX)
        slot = slot_of(i, k)
        return remote(
            xsend.at[slot, part_of(part)], xrecv.at[at, k // 2, part_of(part)],
            ps_sem.at[slot, part], pr_sem.at[at, k // 2, part], (row, group * NX + i),
        )

    def multiply(i, k):
        slot = slot_of(i, k)
        mine = core == lax.rem(k, 2)
        for part in range(PARTS):
            value = lax.dot_general(
                weighted[i + k, :, part * half : (part + 1) * half], weighted[i],
                CROSS_ROWS, preferred_element_type=F32,
            )

            @pl.when(mine)
            def _():
                own[slot, part_of(part)] = value

            @pl.when(jnp.logical_not(mine))
            def _():
                csend[slot, part_of(part)] = value
                swap(slot, part).start()

    def relay(i, k, part):
        slot = slot_of(i, k)
        return remote(
            xsend.at[slot, part_of(part)], between.at[part, k // 2],
            ps_sem.at[slot, part], bs_sem.at[part, k // 2], x_peer(1 if part == 0 else NX - 1),
        )

    def both_cores(slot, part):
        at = part_of(part)
        return own[slot, at] + crecv[slot, at]

    def finish(i, k):
        slot = slot_of(i, k)
        away = lax.rem(i - x + NX, NX)

        @pl.when(core == lax.rem(k, 2))
        def _():
            for part in range(PARTS):
                at = part_of(part)
                swap(slot, part).wait_recv()
                straight = 3 if part == 0 else 1

                @pl.when((away == straight) | (away == 2))
                def _():
                    xsend[slot, at] = both_cores(slot, part).astype(BF16)

                @pl.when(away == straight)
                def _():
                    to_owner(i, k, part).start()

                @pl.when(away == 2)
                def _():
                    relay(i, k, part).start()

                @pl.when((away == 0) | (away == NX - straight))
                def _():
                    own[slot, at] = both_cores(slot, part)

    def pass_sum(part, kk):
        i = x_at[1 if part == 0 else NX - 1]
        k = kk * 2 + core
        slot = slot_of(i, k)
        at = part_of(part)

        @pl.when((i != LAST_PAIR[0]) | (k != LAST_PAIR[1]))
        def _():
            relay(i, k, part).wait_recv()
            xsend[slot, at] = (own[slot, at] + between[part, kk].astype(F32)).astype(BF16)
            to_owner(i, k, part).start()

    last_slot, last_kk = slot_of(*LAST_PAIR), LAST_PAIR[1] // 2
    last_mine = core == LAST_PAIR[1] % 2

    def swap_last(part):
        at = last_part(part)
        return remote(csend.at[last_slot, at], crecv.at[last_slot, at], lcs_sem.at[part], lcr_sem.at[part], partner)

    def last_to_owner(part):
        away = lax.rem(x - LAST_PAIR[0] + NX, NX)
        place = lax.rem(away + NX - 1, NX)
        at = last_part(part)
        return remote(
            xsend.at[last_slot, at], xrecv.at[place, last_kk, at],
            lps_sem.at[part], lpr_sem.at[place, part], (row, group * NX + LAST_PAIR[0]),
        )

    def multiply_last(part):
        i, k = LAST_PAIR
        at = last_part(part)
        value = lax.dot_general(
            weighted[i + k, :, part * thin : (part + 1) * thin], weighted[i],
            CROSS_ROWS, preferred_element_type=F32,
        )

        @pl.when(last_mine)
        def _():
            own[last_slot, at] = value

        @pl.when(jnp.logical_not(last_mine))
        def _():
            csend[last_slot, at] = value
            swap_last(part).start()

    def finish_last(part):
        at = last_part(part)

        @pl.when(last_mine)
        def _():
            swap_last(part).wait_recv()
            value = own[last_slot, at] + crecv[last_slot, at]

            @pl.when(x == LAST_PAIR[0])
            def _():
                own[last_slot, at] = value

            @pl.when(x != LAST_PAIR[0])
            def _():
                xsend[last_slot, at] = value.astype(BF16)
                last_to_owner(part).start()

    def gathered_last(part):
        at = last_part(part)
        value = own[last_slot, at]
        for d in range(NX - 1):
            remote(
                xsend.at[last_slot, at], xrecv.at[d, last_kk, at], lps_sem.at[part], lpr_sem.at[d, part], x_peer(d + 1)
            ).wait_recv()
            value = value + xrecv[d, last_kk, at].astype(F32)
        return value

    def across_last(part):
        at = last_part(part)
        return remote(zsend.at[at], zrecv.at[at], lzs_sem.at[part], lzr_sem.at[part], opposite)

    def take_halo(block, piece):
        forward(block, piece).wait_recv()
        weigh(weighted.at[NX + block], weighted.at[NX + block], piece)

    ahead = jnp.where(x == 2, 1, 0)
    near_pairs = [lag_pair(pairs) for pairs in NEAR_PAIRS]
    next_pairs = [lag_pair(pairs) for pairs in NEXT_PAIRS]
    def take_means():
        for step in range(1, NG):
            send_far(step).wait_recv()
        total = partial[...]
        for step in range(NG - 1):
            total = total + far[step]
        mean = total[:tiles] / (hours * NX * NG)
        spread(lambda a: mean[a : a + 1], means)

    for piece in range(chunks):
        arrival(2, piece).wait_recv()

        @pl.when((x == 2) | (x == 3))
        def _():
            forward(x_at[2], piece).start()
        if not piece:
            take_means()
        weigh(raw.at[x_at[2]], weighted.at[x_at[2]], piece)
        if piece < 4:
            for each in range(piece * 3, piece * 3 + 3):
                for step in (0, 1, 3):
                    weigh(raw.at[x_at[step]], weighted.at[x_at[step]], each)
        elif piece < 10:
            multiply(*near_pairs[piece - 4])
            for each in range(2):
                take_halo(ahead, (piece - 4) * 2 + each)
        else:
            multiply(*next_pairs[piece - 10])
    for part in range(LAST_PARTS):
        for at in range(BANDS):
            if (part, at) not in AHEAD:
                @pl.when(x == 2)
                def _():
                    forward_last(part, at, True).start()

                @pl.when(x != 2)
                def _():
                    forward_last(part, at).start()
            else:
                @pl.when(x < 2)
                def _():
                    forward_last(part, at).start()

    out_pairs = [lag_pair(pairs) for pairs in OUT_PAIRS]
    sent = 0
    for upto, pairs in zip(OUT_AT, (FAR_ORDER, THEN_ORDER, [])):
        for pair in out_pairs[sent:upto]:
            finish(*pair)
        sent = upto
        if pairs is THEN_ORDER:
            for piece in range(chunks):
                take_halo(1 - ahead, piece)
        for each in pairs:
            multiply(*lag_pair(each))
    for kk in (1 - zh, zh):
        for part in range(PARTS):
            pass_sum(part, kk)

    def gathered(kk, part):
        def came(d):
            return remote(
                xsend.at[0, part_of(part)], xrecv.at[d, kk, part_of(part)],
                ps_sem.at[0, part], pr_sem.at[d, kk, part], x_peer(d + 1),
            )

        value = own[x * 2 + kk, part_of(part)]
        for d in (0, 2):
            came(d).wait_recv()
            value = value + xrecv[d, kk, part_of(part)].astype(F32)
        return value

    def across(part):
        return remote(
            zsend.at[part_of(part)], zrecv.at[part_of(part)], zs_sem.at[part], zr_sem.at[part], opposite
        )

    def send_across():
        for part in range(PARTS):
            zsend[part_of(part)] = gathered(1 - zh, part).astype(BF16)
            across(part).start()

    owner = (x == LAST_PAIR[0]) & last_mine & (zh == last_kk)
    sender = (x == LAST_PAIR[0]) & last_mine & (zh != last_kk)
    for part in range(LAST_PARTS):
        for at in range(BANDS):
            forward_last(part, at).wait_recv()
            for piece in range(at * band // CHUNK, (at + 1) * band // CHUNK):
                weigh(weighted.at[NX + 2], weighted.at[NX + 2], piece, part * thin, thin)
        multiply_last(part)
        if part == 1:
            @pl.when(jnp.logical_not(sender))
            def _():
                send_across()
        if part:
            finish_last(part - 1)
    finish_last(LAST_PARTS - 1)

    @pl.when(sender)
    def _():
        for part in range(LAST_PARTS):
            zsend[last_part(part)] = gathered_last(part).astype(BF16)
            across_last(part).start()

    divisor = math.sqrt(quarter * NX * 4)

    @pl.when(owner)
    def _():
        for part in range(LAST_PARTS):
            at = last_part(part)
            value = gathered_last(part)
            across_last(part).wait_recv()
            out[at] = (value + zrecv[at].astype(F32)) / divisor

    @pl.when(jnp.logical_not(owner))
    def _():
        for part in range(PARTS):
            at = part_of(part)
            value = gathered(zh, part)
            across(part).wait_recv()
            out[at] = (value + zrecv[at].astype(F32)) / divisor

    for step in range(1, NX):
        for piece in range(chunks):
            exchange(step, piece).wait_send()
        send_near(step).wait_send()
    for step in range(1, NG):
        send_far(step).wait_send()
    for block in range(NX - 2):
        for piece in range(chunks):
            forward(block, piece).wait_send()
    for part in range(LAST_PARTS):
        for at in range(BANDS):
            forward_last(part, at).wait_send()
    for i in range(NX):
        for k in range(LAGS):
            if (i, k) == LAST_PAIR:
                continue
            for part in range(PARTS):
                @pl.when(core != k % 2)
                def _():
                    swap(slot_of(i, k), part).wait_send()

                @pl.when((core == k % 2) & (x != i))
                def _():
                    to_owner(i, k, part).wait_send()
    for part in range(LAST_PARTS):
        @pl.when(jnp.logical_not(last_mine))
        def _():
            swap_last(part).wait_send()

        @pl.when(last_mine & (x != LAST_PAIR[0]))
        def _():
            last_to_owner(part).wait_send()

        @pl.when(sender)
        def _():
            across_last(part).wait_send()
    for part in range(PARTS):
        @pl.when(jnp.logical_not(sender))
        def _():
            across(part).wait_send()


def body(temps, area, ocean_rows, counts):
    rows, hours = temps.shape
    quarter = rows // NX
    chunks = quarter // CHUNK
    vmem = pl.BlockSpec(memory_space=pltpu.VMEM)
    any_space = pl.BlockSpec(memory_space=pl.ANY)
    dma = pltpu.SemaphoreType.DMA
    return pl.pallas_call(
        kernel,
        out_shape=pltpu.VMEM((hours, hours), F32),
        in_specs=[
            any_space, any_space, any_space, pl.BlockSpec(memory_space=pltpu.SMEM),
        ],
        out_specs=vmem,
        scratch_shapes=[
            pltpu.VMEM((NX, quarter, hours), BF16),
            pltpu.VMEM((2 * NX - 1, quarter, hours), BF16),
            pltpu.VMEM((2 * NX, hours, hours), F32),
            pltpu.VMEM((2 * NX, hours, hours), F32),
            pltpu.VMEM((2 * NX, hours, hours), F32),
            pltpu.VMEM((2 * NX, hours, hours), BF16),
            pltpu.VMEM((NX - 1, 2, hours, hours), BF16),
            pltpu.VMEM((PARTS, 2, hours // PARTS, hours), BF16),
            pltpu.VMEM((hours, hours), BF16),
            pltpu.VMEM((hours, hours), BF16),
            pltpu.VMEM((NX, 16, LANES), F32),
            pltpu.VMEM((NX - 1, 16, LANES), F32),
            pltpu.VMEM((16, LANES), F32),
            pltpu.VMEM((NG - 1, 16, LANES), F32),
            pltpu.VMEM((rows // LANES, LANES), F32),
            pltpu.VMEM((rows // LANES, LANES), jnp.int32),
            pltpu.VMEM((rows // LANES, LANES), F32),
            pltpu.VMEM((quarter, LANES), F32),
            pltpu.VMEM((quarter, LANES), F32),
            dma((NX + 3,)),
            dma((NX - 1, chunks)), dma((NX - 1, chunks)),
            dma((NX - 2, chunks)), dma((NX - 2, chunks)),
            dma((LAST_PARTS, BANDS)), dma((LAST_PARTS, BANDS)),
            dma((2 * NX, PARTS)), dma((2 * NX, PARTS)),
            dma((2 * NX, PARTS)), dma((NX - 1, 2, PARTS)), dma((PARTS, 2)),
            dma((PARTS,)), dma((PARTS,)),
            dma((NX - 1,)), dma((NX - 1,)),
            dma((NG - 1,)), dma((NG - 1,)),
            dma((LAST_PARTS,)), dma((LAST_PARTS,)),
            dma((LAST_PARTS,)), dma((NX - 1, LAST_PARTS)),
            dma((LAST_PARTS,)), dma((LAST_PARTS,)),
        ],
        compiler_params=pltpu.CompilerParams(
            collective_id=0, has_side_effects=True, vmem_limit_bytes=56 << 20
        ),
        cost_estimate=pl.CostEstimate(
            flops=2 * LAGS * hours * hours * rows, bytes_accessed=2 * rows * hours, transcendentals=0
        ),
        name="lagged_band",
    )(temps, area.reshape(-1, LANES), ocean_rows.reshape(-1, LANES), counts)


def solution(mesh):
    in_specs = (P("row", "tm"), P("row"), P("row"), P("row"))
    out_specs = P("row", "tm")
    return jax.shard_map(body, mesh=mesh, in_specs=in_specs, out_specs=out_specs, check_vma=False)
```

```python
import functools
import math

import jax
import jax.numpy as jnp
from jax import lax
from jax.experimental import pallas as pl
from jax.experimental.pallas import tpu as pltpu
from jax.sharding import PartitionSpec as P

LAGS = 4
NX = 4
NG = 8
LANES = 128
CHUNK = 128
EARLY = 2
WINDOW = 6
BANDS = 3
AHEAD = ((0, 0), (1, 0), (0, 1))
LAST_PARTS = 4
MESH = pl.DeviceIdType.MESH
F32 = jnp.float32
BF16 = jnp.bfloat16
CROSS_ROWS = (((0,), (0,)), ((), ()))
CROSS_LANES = (((1,), (1,)), ((), ()))
PARTS = 2


NEAR_PAIRS = list(zip(
    [(1, 0), (3, 0), (1, 2), (0, 0), (0, 1), (0, 3)],
    [(0, 0), (2, 0), (0, 1), (0, 2), (1, 0), (1, 1)],
    [(1, 0), (3, 0), (1, 1), (1, 2), (2, 0), (2, 1)],
    [(0, 0), (2, 0), (0, 2), (2, 1), (0, 3), (3, 0)],
))
NEXT_PAIRS = list(zip(
    [(3, 1), (1, 3)],
    [(2, 2), (1, 3)],
    [(3, 2), (2, 3)],
    [(2, 2), (3, 1)],
))
FAR_PAIRS = list(zip(
    [(2, 0), (2, 1), (1, 1), (0, 2)],
    [(3, 0), (2, 1), (0, 3), (1, 2)],
    [(0, 0), (0, 1), (0, 2), (0, 3)],
    [(1, 0), (1, 1), (0, 1), (1, 2)],
))
THEN_PAIRS = list(zip(
    [(2, 2), (3, 2), (2, 3)],
    [(3, 1), (2, 3), (3, 2)],
    [(1, 3), (3, 1), (2, 2)],
    [(1, 3), (2, 3), (3, 2)],
))
LAST_PAIR = (3, 3)
OUT_AT = (5, 12, 15)


def crossing_first(pairs, zh):
    return sorted(pairs, key=lambda pair: pair[1] // 2 == zh)


def out_order(zh, x):
    def best(pool, taken):
        def rank(pair):
            i, k = pair
            since = [n for n, (owner, _) in enumerate(taken) if owner == i]
            return (i == x, k // 2 == zh, since[-1] if since else -1, pool.index(pair))

        return min(pool, key=rank)

    pool = [pairs[x] for pairs in NEAR_PAIRS + NEXT_PAIRS]
    taken = []
    for upto, more in zip(OUT_AT, (FAR_PAIRS, THEN_PAIRS, [])):
        while len(taken) < upto:
            pair = best(pool, taken)
            pool.remove(pair)
            taken.append(pair)
        pool += [pairs[x] for pairs in more]
    return taken


def by_place(order):
    return list(zip(*[order(zh, x) for zh in range(2) for x in range(NX)]))


OUT_PAIRS = by_place(out_order)
FAR_ORDER = by_place(lambda zh, x: crossing_first([pairs[x] for pairs in FAR_PAIRS], zh))
THEN_ORDER = by_place(lambda zh, x: crossing_first([pairs[x] for pairs in THEN_PAIRS], zh))


def kernel(
    temps, area_in, listed_in, count, out,
    raw, weighted, own, csend, crecv, xsend, xrecv, between, zsend, zrecv,
    sums, near, partial, far, area, listed, scale, means, scales, local_sem,
    xs_sem, xr_sem, hs_sem, hr_sem, ls_sem, lr_sem, cs_sem, cr_sem, ps_sem, pr_sem, bs_sem, zs_sem, zr_sem,
    ns_sem, nr_sem, fs_sem, fr_sem,
    lcs_sem, lcr_sem, lps_sem, lpr_sem, lzs_sem, lzr_sem,
):
    row, tm = lax.axis_index("row"), lax.axis_index("tm")
    zh, core = row // 2, lax.rem(row, 2)
    group, x = tm // NX, lax.rem(tm, NX)
    quarter = raw.shape[1]
    chunks = quarter // CHUNK
    tiles = quarter // LANES
    hours = raw.shape[2]
    half = hours // PARTS

    def x_peer(step):
        return (row, group * NX + lax.rem(x + step, NX))

    def g_peer(step):
        return (row, lax.rem(group + step, NG) * NX + x)

    partner = (zh * 2 + 1 - core, tm)
    opposite = (lax.rem(row + 2, 4), tm)
    x_at = [lax.rem(x + step, NX) for step in range(NX)]

    barrier = pltpu.get_barrier_semaphore()
    everyone = [x_peer(s) for s in range(1, NX)] + [g_peer(s) for s in range(1, NG)]
    everyone += [partner, opposite]
    for device in everyone:
        pl.semaphore_signal(barrier, inc=1, device_id=device, device_id_type=MESH)

    def remote(src, dst, send, recv, device):
        return pltpu.make_async_remote_copy(
            src_ref=src, dst_ref=dst, send_sem=send, recv_sem=recv, device_id=device, device_id_type=MESH
        )

    def rows_of(piece, base=0):
        return pl.ds(pl.multiple_of(base + piece * CHUNK, CHUNK), CHUNK)

    stage = [
        pltpu.make_async_copy(
            temps.at[pl.ds(q * quarter, quarter)], weighted.at[q], local_sem.at[q]
        )
        for q in range(NX)
    ]
    keep = pltpu.make_async_copy(
        temps.at[pl.ds(pl.multiple_of(x * quarter, quarter), quarter)], raw.at[x], local_sem.at[NX]
    )
    for copy in stage:
        copy.start()
    keep.start()
    tables = [
        pltpu.make_async_copy(area_in, area, local_sem.at[NX + 1]),
        pltpu.make_async_copy(listed_in, listed, local_sem.at[NX + 2]),
    ]
    for copy in tables:
        copy.start()

    def exchange(step, piece):
        target = x_at[step]
        return remote(
            temps.at[rows_of(piece, target * quarter)], raw.at[x, rows_of(piece)],
            xs_sem.at[step - 1, piece], xr_sem.at[NX - step - 1, piece], x_peer(step),
        )

    def arrival(step, piece):
        source = x_at[step]
        return remote(
            temps.at[rows_of(piece)], raw.at[source, rows_of(piece)],
            xs_sem.at[0, 0], xr_sem.at[step - 1, piece], x_peer(step),
        )

    def forward(block, piece):
        return remote(
            raw.at[block, rows_of(piece)], weighted.at[NX + block, rows_of(piece)],
            hs_sem.at[block, piece], hr_sem.at[block, piece], g_peer(NG - 1),
        )

    def forward_own(piece):
        return remote(
            temps.at[rows_of(piece, x * quarter)], weighted.at[NX + x, rows_of(piece)],
            hs_sem.at[x, piece], hr_sem.at[x, piece], g_peer(NG - 1),
        )

    band = quarter // BANDS
    thin = hours // LAST_PARTS

    def last_part(part):
        return pl.ds(part * thin, thin)

    def forward_last(part, at, mine=False):
        r, cols = pl.ds(at * band, band), last_part(part)
        source = raw.at[2, r, cols]
        if mine:
            source = temps.at[pl.ds(pl.multiple_of(x * quarter + at * band, band), band), cols]
        return remote(
            source, weighted.at[NX + 2, r, cols], ls_sem.at[part, at], lr_sem.at[part, at], g_peer(NG - 1)
        )

    pl.semaphore_wait(barrier, len(everyone))

    for piece in range(WINDOW):
        exchange(3, piece).start()
        exchange(1, piece).start()
        if piece < EARLY:
            @pl.when(x < 2)
            def _():
                forward_own(piece).start()
    for piece in range(EARLY, chunks):
        @pl.when(x == 0)
        def _():
            forward_own(piece).start()

    @pl.when(x == 2)
    def _():
        for part, at in AHEAD:
            forward_last(part, at, True).start()

    def send_near(step):
        return remote(
            sums.at[x_at[step]], near.at[NX - step - 1], ns_sem.at[step - 1], nr_sem.at[NX - step - 1], x_peer(step)
        )

    def send_far(step):
        return remote(partial, far.at[NG - step - 1], fs_sem.at[step - 1], fr_sem.at[NG - step - 1], g_peer(step))

    def one_hop(piece):
        @pl.when(x == 3)
        def _():
            arrival(1, piece).wait_recv()
            forward(0, piece).start()
            arrival(3, piece).wait_recv()

        @pl.when(x != 3)
        def _():
            arrival(3, piece).wait_recv()

            @pl.when(x != 0)
            def _():
                forward(x - 1, piece).start()
            arrival(1, piece).wait_recv()

        for part, at in AHEAD:
            if (piece + 1) * CHUNK == (at + 1) * band:
                @pl.when(x == 3)
                def _():
                    forward_last(part, at).start()
        if piece + WINDOW < chunks:
            exchange(1, piece + WINDOW).start()
            exchange(3, piece + WINDOW).start()
        else:
            some = chunks // WINDOW
            for late in range(some):
                exchange(2, (piece + WINDOW - chunks) * some + late).start()

    one_hop(0)
    one_hop(1)

    sums[...] = jnp.zeros_like(sums)
    ones = jnp.ones((8, hours), BF16)
    for q in range(NX):
        stage[q].wait()
        for piece in range(quarter // 512):
            some = lax.dot_general(
                ones, weighted[q, pl.ds(piece * 512, 512)], CROSS_LANES, preferred_element_type=F32
            )
            for part in range(4):
                sums[q, pl.ds(piece * 4 + part, 1)] = some[0:1, part * LANES : (part + 1) * LANES]
        if q < 3:
            one_hop(q + 2)
    keep.wait()
    for copy in tables:
        copy.wait()
    for step in range(1, NX):
        send_near(step).start()

    live = count[0]
    groups = listed.shape[0]

    def mark(part, mask):
        value = listed[pl.ds(part, 1), :]
        high = jnp.broadcast_to(value // LANES, (groups, LANES))
        low = jnp.broadcast_to(value % LANES, (LANES, LANES))
        place = lax.broadcasted_iota(jnp.int32, (LANES, LANES), 1) + part * LANES
        left = jnp.where(high == lax.broadcasted_iota(jnp.int32, (groups, LANES), 0), 1.0, 0.0).astype(BF16)
        hit = (low == lax.broadcasted_iota(jnp.int32, (LANES, LANES), 0)) & (place < live)
        right = jnp.where(hit, 1.0, 0.0).astype(BF16)
        return mask + lax.dot_general(left, right, CROSS_LANES, preferred_element_type=F32)

    mask = jnp.zeros((groups, LANES), F32)
    for q in range(4):
        mask = lax.fori_loop(q * (groups // 4), (q + 1) * (groups // 4), mark, mask)
        one_hop(5 + q)
    scale[...] = mask * area[...]

    def spread(row_of, target):
        for a in range(tiles):
            target[pl.ds(a * LANES, LANES)] = jnp.broadcast_to(row_of(a), (LANES, LANES)).T

    for step in range(1, NX):
        send_near(step).wait_recv()
    partial[...] = sums[x] + near[0] + near[1] + near[2]
    for step in range(1, NG):
        send_far(step).start()
    one_hop(9)
    spread(lambda a: scale[pl.ds(x * tiles + a, 1)], scales)
    for piece in range(10, chunks):
        one_hop(piece)

    for piece in range(chunks):
        @pl.when(x == 0)
        def _():
            forward(1, piece).start()
        if piece >= EARLY:
            @pl.when(x == 1)
            def _():
                forward_own(piece).start()

    def weigh(source, target, piece, first=0, size=None):
        r = rows_of(piece)
        m, s = means[r], scales[r]
        for lane in range(first, first + (size or hours), LANES):
            at = pl.ds(lane, LANES)
            target[r, at] = ((source[r, at].astype(F32) - m) * s).astype(BF16)

    def pick(values):
        at = x if len(values) == NX else zh * NX + x
        value = values[0]
        for n in range(1, len(values)):
            value = jnp.where(at == n, values[n], value)
        return value

    def lag_pair(pairs):
        return pick([i for i, _ in pairs]), pick([k for _, k in pairs])

    def slot_of(i, k):
        return i * 2 + k // 2

    def part_of(part):
        return pl.ds(part * half, half)

    def swap(slot, part):
        return remote(
            csend.at[slot, part_of(part)], crecv.at[slot, part_of(part)],
            cs_sem.at[slot, part], cr_sem.at[slot, part], partner,
        )

    def to_owner(i, k, part):
        away = lax.rem(x - i + NX, NX)
        at = lax.rem(away + NX - 1, NX)
        slot = slot_of(i, k)
        return remote(
            xsend.at[slot, part_of(part)], xrecv.at[at, k // 2, part_of(part)],
            ps_sem.at[slot, part], pr_sem.at[at, k // 2, part], (row, group * NX + i),
        )

    def multiply(i, k):
        slot = slot_of(i, k)
        mine = core == lax.rem(k, 2)
        for part in range(PARTS):
            value = lax.dot_general(
                weighted[i + k, :, part * half : (part + 1) * half], weighted[i],
                CROSS_ROWS, preferred_element_type=F32,
            )

            @pl.when(mine)
            def _():
                own[slot, part_of(part)] = value

            @pl.when(jnp.logical_not(mine))
            def _():
                csend[slot, part_of(part)] = value
                swap(slot, part).start()

    def relay(i, k, part):
        slot = slot_of(i, k)
        return remote(
            xsend.at[slot, part_of(part)], between.at[part, k // 2],
            ps_sem.at[slot, part], bs_sem.at[part, k // 2], x_peer(1 if part == 0 else NX - 1),
        )

    def both_cores(slot, part):
        at = part_of(part)
        return own[slot, at] + crecv[slot, at]

    def finish(i, k):
        slot = slot_of(i, k)
        away = lax.rem(i - x + NX, NX)

        @pl.when(core == lax.rem(k, 2))
        def _():
            for part in range(PARTS):
                at = part_of(part)
                swap(slot, part).wait_recv()
                straight = 3 if part == 0 else 1

                @pl.when((away == straight) | (away == 2))
                def _():
                    xsend[slot, at] = both_cores(slot, part).astype(BF16)

                @pl.when(away == straight)
                def _():
                    to_owner(i, k, part).start()

                @pl.when(away == 2)
                def _():
                    relay(i, k, part).start()

                @pl.when((away == 0) | (away == NX - straight))
                def _():
                    own[slot, at] = both_cores(slot, part)

    def pass_sum(part, kk):
        i = x_at[1 if part == 0 else NX - 1]
        k = kk * 2 + core
        slot = slot_of(i, k)
        at = part_of(part)

        @pl.when((i != LAST_PAIR[0]) | (k != LAST_PAIR[1]))
        def _():
            relay(i, k, part).wait_recv()
            xsend[slot, at] = (own[slot, at] + between[part, kk].astype(F32)).astype(BF16)
            to_owner(i, k, part).start()

    last_slot, last_kk = slot_of(*LAST_PAIR), LAST_PAIR[1] // 2
    last_mine = core == LAST_PAIR[1] % 2

    def swap_last(part):
        at = last_part(part)
        return remote(csend.at[last_slot, at], crecv.at[last_slot, at], lcs_sem.at[part], lcr_sem.at[part], partner)

    def last_to_owner(part):
        away = lax.rem(x - LAST_PAIR[0] + NX, NX)
        place = lax.rem(away + NX - 1, NX)
        at = last_part(part)
        return remote(
            xsend.at[last_slot, at], xrecv.at[place, last_kk, at],
            lps_sem.at[part], lpr_sem.at[place, part], (row, group * NX + LAST_PAIR[0]),
        )

    def multiply_last(part):
        i, k = LAST_PAIR
        at = last_part(part)
        value = lax.dot_general(
            weighted[i + k, :, part * thin : (part + 1) * thin], weighted[i],
            CROSS_ROWS, preferred_element_type=F32,
        )

        @pl.when(last_mine)
        def _():
            own[last_slot, at] = value

        @pl.when(jnp.logical_not(last_mine))
        def _():
            csend[last_slot, at] = value
            swap_last(part).start()

    def finish_last(part):
        at = last_part(part)

        @pl.when(last_mine)
        def _():
            swap_last(part).wait_recv()
            value = own[last_slot, at] + crecv[last_slot, at]

            @pl.when(x == LAST_PAIR[0])
            def _():
                own[last_slot, at] = value

            @pl.when(x != LAST_PAIR[0])
            def _():
                xsend[last_slot, at] = value.astype(BF16)
                last_to_owner(part).start()

    def gathered_last(part):
        at = last_part(part)
        value = own[last_slot, at]
        for d in range(NX - 1):
            remote(
                xsend.at[last_slot, at], xrecv.at[d, last_kk, at], lps_sem.at[part], lpr_sem.at[d, part], x_peer(d + 1)
            ).wait_recv()
            value = value + xrecv[d, last_kk, at].astype(F32)
        return value

    def across_last(part):
        at = last_part(part)
        return remote(zsend.at[at], zrecv.at[at], lzs_sem.at[part], lzr_sem.at[part], opposite)

    def take_halo(block, piece):
        forward(block, piece).wait_recv()
        weigh(weighted.at[NX + block], weighted.at[NX + block], piece)

    ahead = jnp.where(x == 2, 1, 0)
    near_pairs = [lag_pair(pairs) for pairs in NEAR_PAIRS]
    next_pairs = [lag_pair(pairs) for pairs in NEXT_PAIRS]
    def take_means():
        for step in range(1, NG):
            send_far(step).wait_recv()
        total = partial[...]
        for step in range(NG - 1):
            total = total + far[step]
        mean = total[:tiles] / (hours * NX * NG)
        spread(lambda a: mean[a : a + 1], means)

    for piece in range(chunks):
        arrival(2, piece).wait_recv()

        @pl.when((x == 2) | (x == 3))
        def _():
            forward(x_at[2], piece).start()
        if not piece:
            take_means()
        weigh(raw.at[x_at[2]], weighted.at[x_at[2]], piece)
        if piece < 4:
            for each in range(piece * 3, piece * 3 + 3):
                for step in (0, 1, 3):
                    weigh(raw.at[x_at[step]], weighted.at[x_at[step]], each)
        elif piece < 10:
            multiply(*near_pairs[piece - 4])
            for each in range(2):
                take_halo(ahead, (piece - 4) * 2 + each)
        else:
            multiply(*next_pairs[piece - 10])
    for part in range(LAST_PARTS):
        for at in range(BANDS):
            if (part, at) not in AHEAD:
                @pl.when(x == 2)
                def _():
                    forward_last(part, at, True).start()

                @pl.when(x != 2)
                def _():
                    forward_last(part, at).start()
            else:
                @pl.when(x < 2)
                def _():
                    forward_last(part, at).start()

    out_pairs = [lag_pair(pairs) for pairs in OUT_PAIRS]
    sent = 0
    for upto, pairs in zip(OUT_AT, (FAR_ORDER, THEN_ORDER, [])):
        for pair in out_pairs[sent:upto]:
            finish(*pair)
        sent = upto
        if pairs is THEN_ORDER:
            for piece in range(chunks):
                take_halo(1 - ahead, piece)
        for each in pairs:
            multiply(*lag_pair(each))
    for kk in (1 - zh, zh):
        for part in range(PARTS):
            pass_sum(part, kk)

    def gathered(kk, part):
        def came(d):
            return remote(
                xsend.at[0, part_of(part)], xrecv.at[d, kk, part_of(part)],
                ps_sem.at[0, part], pr_sem.at[d, kk, part], x_peer(d + 1),
            )

        value = own[x * 2 + kk, part_of(part)]
        for d in (0, 2):
            came(d).wait_recv()
            value = value + xrecv[d, kk, part_of(part)].astype(F32)
        return value

    def across(part):
        return remote(
            zsend.at[part_of(part)], zrecv.at[part_of(part)], zs_sem.at[part], zr_sem.at[part], opposite
        )

    def send_across():
        for part in range(PARTS):
            zsend[part_of(part)] = gathered(1 - zh, part).astype(BF16)
            across(part).start()

    owner = (x == LAST_PAIR[0]) & last_mine & (zh == last_kk)
    sender = (x == LAST_PAIR[0]) & last_mine & (zh != last_kk)
    for part in range(LAST_PARTS):
        for at in range(BANDS):
            forward_last(part, at).wait_recv()
            for piece in range(at * band // CHUNK, (at + 1) * band // CHUNK):
                weigh(weighted.at[NX + 2], weighted.at[NX + 2], piece, part * thin, thin)
        multiply_last(part)
        if part == 1:
            @pl.when(jnp.logical_not(sender))
            def _():
                send_across()
        if part:
            finish_last(part - 1)
    finish_last(LAST_PARTS - 1)

    @pl.when(sender)
    def _():
        for part in range(LAST_PARTS):
            zsend[last_part(part)] = gathered_last(part).astype(BF16)
            across_last(part).start()

    divisor = math.sqrt(quarter * NX * 4)

    @pl.when(owner)
    def _():
        for part in range(LAST_PARTS):
            at = last_part(part)
            value = gathered_last(part)
            across_last(part).wait_recv()
            out[at] = (value + zrecv[at].astype(F32)) / divisor

    @pl.when(jnp.logical_not(owner))
    def _():
        for part in range(PARTS):
            at = part_of(part)
            value = gathered(zh, part)
            across(part).wait_recv()
            out[at] = (value + zrecv[at].astype(F32)) / divisor

    for step in range(1, NX):
        for piece in range(chunks):
            exchange(step, piece).wait_send()
        send_near(step).wait_send()
    for step in range(1, NG):
        send_far(step).wait_send()
    for block in range(NX - 2):
        for piece in range(chunks):
            forward(block, piece).wait_send()
    for part in range(LAST_PARTS):
        for at in range(BANDS):
            forward_last(part, at).wait_send()
    for i in range(NX):
        for k in range(LAGS):
            if (i, k) == LAST_PAIR:
                continue
            for part in range(PARTS):
                @pl.when(core != k % 2)
                def _():
                    swap(slot_of(i, k), part).wait_send()

                @pl.when((core == k % 2) & (x != i))
                def _():
                    to_owner(i, k, part).wait_send()
    for part in range(LAST_PARTS):
        @pl.when(jnp.logical_not(last_mine))
        def _():
            swap_last(part).wait_send()

        @pl.when(last_mine & (x != LAST_PAIR[0]))
        def _():
            last_to_owner(part).wait_send()

        @pl.when(sender)
        def _():
            across_last(part).wait_send()
    for part in range(PARTS):
        @pl.when(jnp.logical_not(sender))
        def _():
            across(part).wait_send()


def body(temps, area, ocean_rows, counts):
    rows, hours = temps.shape
    quarter = rows // NX
    chunks = quarter // CHUNK
    vmem = pl.BlockSpec(memory_space=pltpu.VMEM)
    any_space = pl.BlockSpec(memory_space=pl.ANY)
    dma = pltpu.SemaphoreType.DMA
    return pl.pallas_call(
        kernel,
        out_shape=pltpu.VMEM((hours, hours), F32),
        in_specs=[
            any_space, any_space, any_space, pl.BlockSpec(memory_space=pltpu.SMEM),
        ],
        out_specs=vmem,
        scratch_shapes=[
            pltpu.VMEM((NX, quarter, hours), BF16),
            pltpu.VMEM((2 * NX - 1, quarter, hours), BF16),
            pltpu.VMEM((2 * NX, hours, hours), F32),
            pltpu.VMEM((2 * NX, hours, hours), F32),
            pltpu.VMEM((2 * NX, hours, hours), F32),
            pltpu.VMEM((2 * NX, hours, hours), BF16),
            pltpu.VMEM((NX - 1, 2, hours, hours), BF16),
            pltpu.VMEM((PARTS, 2, hours // PARTS, hours), BF16),
            pltpu.VMEM((hours, hours), BF16),
            pltpu.VMEM((hours, hours), BF16),
            pltpu.VMEM((NX, 16, LANES), F32),
            pltpu.VMEM((NX - 1, 16, LANES), F32),
            pltpu.VMEM((16, LANES), F32),
            pltpu.VMEM((NG - 1, 16, LANES), F32),
            pltpu.VMEM((rows // LANES, LANES), F32),
            pltpu.VMEM((rows // LANES, LANES), jnp.int32),
            pltpu.VMEM((rows // LANES, LANES), F32),
            pltpu.VMEM((quarter, LANES), F32),
            pltpu.VMEM((quarter, LANES), F32),
            dma((NX + 3,)),
            dma((NX - 1, chunks)), dma((NX - 1, chunks)),
            dma((NX - 2, chunks)), dma((NX - 2, chunks)),
            dma((LAST_PARTS, BANDS)), dma((LAST_PARTS, BANDS)),
            dma((2 * NX, PARTS)), dma((2 * NX, PARTS)),
            dma((2 * NX, PARTS)), dma((NX - 1, 2, PARTS)), dma((PARTS, 2)),
            dma((PARTS,)), dma((PARTS,)),
            dma((NX - 1,)), dma((NX - 1,)),
            dma((NG - 1,)), dma((NG - 1,)),
            dma((LAST_PARTS,)), dma((LAST_PARTS,)),
            dma((LAST_PARTS,)), dma((NX - 1, LAST_PARTS)),
            dma((LAST_PARTS,)), dma((LAST_PARTS,)),
        ],
        compiler_params=pltpu.CompilerParams(
            collective_id=0, has_side_effects=True, vmem_limit_bytes=56 << 20
        ),
        cost_estimate=pl.CostEstimate(
            flops=2 * LAGS * hours * hours * rows, bytes_accessed=2 * rows * hours, transcendentals=0
        ),
        name="lagged_band",
    )(temps, area.reshape(-1, LANES), ocean_rows.reshape(-1, LANES), counts)


def solution(mesh):
    in_specs = (P("row", "tm"), P("row"), P("row"), P("row"))
    out_specs = P("row", "tm")
    return jax.shard_map(body, mesh=mesh, in_specs=in_specs, out_specs=out_specs, check_vma=False)
```
